1024 devices in a mesh: blk: 64 (over z_lo, y, core), group: 16 (over x, z_hi).
Axes of the slice: x: 4, y: 4, z: 32 (z_hi: 4, z_lo: 8; z = z_hi * 8 + z_lo), core: 2. Of those that a mesh axis runs over, the one named last changes fastest.
Arguments:
- picture_features_unnormed: float32 [196608, 768], P(('blk', 'group')), may hold values from -0.34280172 to 0.34280172, as said below
- caption_features_unnormed: float32 [196608, 768], P(('blk', 'group')), may hold values from -0.34280172 to 0.34280172, as said below
- example_match_key: int32 [196608], P(('blk', 'group')), may hold values from 0 to 24575, as said below
- picture_loss_share: float32 [196608], P(('blk', 'group')), may hold values from 0.6 to 45, as said below
- score_multiplier: float32 [1], replicated, may hold values from 5 to 15
- score_shift: float32 [1], replicated, may hold values from -5 to -3
Outputs:
- loss: float32 [1], replicated
- image_grad: float32 [196608, 768], P(('blk', 'group'))
- text_grad: float32 [196608, 768], P(('blk', 'group'))
The draws below stay inside these ranges and needn't reach their ends.
Inputs may be any that keep to these rules, and one draw needn't show every extreme that they name: `picture_features_unnormed`: each row is the sum of a part shared by the image and the text of the same sample and a part of its own, times a row scale. `caption_features_unnormed`: each row is the sum of a part shared by the image and the text of the same sample and a part of its own, times a row scale. `example_match_key`: ids may repeat, also over all 192 samples of one device. `picture_loss_share`: positive.
All inputs are finite; a program needn't handle non-finite values.
Results may differ from the reference program's by a relative error of at most 0.0041.
Values may be sent and summed in bfloat16 or wider, within the bound.
No kernel may reach another device: no remote copies, remote signals or barrier semaphores. Data moves between devices by JAX's collectives and lax.ppermute only.
A program may use at most 32 MiB of HBM per device.

```python
import math
import jax
import jax.numpy as jnp
from jax import lax

D = 768
ROWS = 192
STEPS = 8
BATCH = 196608
N_BLK = 64
N_GROUP = 16


def shared_base(key):
    return jnp.clip(jax.random.normal(key, (BATCH, D), jnp.float32), -5.0, 5.0)


def embedding(key, shared_terms):
    noise_key, scale_key = jax.random.split(key)
    place = (jnp.arange(BATCH).astype(jnp.float32) / (BATCH - 1)).reshape(BATCH, 1)
    own_share = 0.3 + 1.5 * place
    jitter = jnp.clip(jax.random.normal(noise_key, (BATCH, D), jnp.float32), -5.0, 5.0)
    mixed = (shared_terms + own_share * jitter) / (1.0 + own_share)
    row_scale = jnp.exp(jax.random.uniform(scale_key, (BATCH, 1), jnp.float32, math.log(0.1), 0.0))
    return mixed * row_scale / math.sqrt(D)


def draw_picture_features_unnormed(key, part):
    shared_terms = shared_base(key)
    key = jax.random.fold_in(key, 1)
    return embedding(key, shared_terms)


def draw_caption_features_unnormed(key, part):
    shared_terms = shared_base(key)
    key = jax.random.fold_in(key, 2)
    return embedding(key, shared_terms)


def draw_example_match_key(key, part):
    key = jax.random.fold_in(key, 4)
    id_key, pick_key, block_key, end_key = jax.random.split(key, 4)
    blocks = BATCH // ROWS
    row_ids = jax.random.randint(id_key, (blocks, ROWS), 0, BATCH // 8)
    picked = jax.random.randint(pick_key, (blocks, 1), 0, 16) == 0
    block_ids = jax.random.randint(block_key, (blocks, 1), 0, BATCH // 8)
    merged = jnp.where(picked, block_ids, row_ids).reshape(BATCH)
    first_end = jax.random.randint(end_key, (), 0, BATCH)
    second_end = (first_end + BATCH // 2) % BATCH
    position = jnp.arange(BATCH)
    merged = jnp.where(position == first_end, BATCH // 8 - 1, merged)
    merged = jnp.where(position == second_end, 0, merged)
    return merged.astype(jnp.int32)


def draw_picture_loss_share(key, part):
    key = jax.random.fold_in(key, 3)
    row_key, block_key = jax.random.split(key)
    place = jnp.arange(BATCH).astype(jnp.float32) / (BATCH - 1)
    blocks = BATCH // ROWS
    block_factor = jnp.exp(jax.random.uniform(block_key, (blocks, 1), jnp.float32, 0.0, math.log(3.0)))
    block_factor = jnp.broadcast_to(block_factor, (blocks, ROWS)).reshape(BATCH)
    rising = 1.0 + 2.0 * place
    spread = jnp.exp(jax.random.uniform(row_key, (BATCH,), jnp.float32, -0.5, 0.5))
    return rising * spread * block_factor


def setup_inputs(seed: int = 0) -> dict:
    splits = jax.random.split(jax.random.key(seed), 7)
    picture_features_unnormed = draw_picture_features_unnormed(jax.random.fold_in(splits[6], 71), 0)
    caption_features_unnormed = draw_caption_features_unnormed(jax.random.fold_in(splits[6], 71), 0)
    example_match_key = draw_example_match_key(jax.random.fold_in(splits[6], 71), 0)
    picture_loss_share = draw_picture_loss_share(jax.random.fold_in(splits[6], 71), 0)
    score_multiplier = jnp.clip(jnp.exp(jax.random.uniform(splits[4], (1,), jnp.float32, math.log(5.0), math.log(15.0))), 5.0, 15.0)
    score_shift = jnp.clip(jax.random.uniform(splits[5], (1,), jnp.float32, -5.0, -3.0), -5.0, -3.0)
    return {"picture_features_unnormed": picture_features_unnormed, "caption_features_unnormed": caption_features_unnormed, "example_match_key": example_match_key, "picture_loss_share": picture_loss_share, "score_multiplier": score_multiplier, "score_shift": score_shift}


def normalize(values):
    row_norm = jnp.sqrt(lax.optimization_barrier(jnp.sum(values * values, -1, keepdims=True)) + 1e-06)
    return (values / row_norm, row_norm)

def match_contributions(picture_features_halfwidth, loss_shares, picture_match_keys, caption_features_halfwidth, caption_match_keys, score_scaled_factor, shifted_scores):
    similarity_matrix = jnp.einsum('bgrd,bgsd->bgrs', picture_features_halfwidth.astype(jnp.float32), caption_features_halfwidth.astype(jnp.float32), precision=lax.Precision.HIGHEST)
    score_matrix = score_scaled_factor * similarity_matrix + shifted_scores
    target_signs = jnp.where(picture_match_keys[..., :, None] == caption_match_keys[..., None, :], 1.0, -1.0).astype(jnp.float32)
    per_line_penalty = lax.optimization_barrier(jnp.sum(jax.nn.softplus(-target_signs * score_matrix), -1))
    multiplier_entry = (loss_shares[..., :, None] * score_scaled_factor * -target_signs * jax.nn.sigmoid(-target_signs * score_matrix)).astype(jnp.bfloat16)
    coef_wide = multiplier_entry.astype(jnp.float32)
    picture_derivative = jnp.einsum('bgrs,bgsd->bgrd', coef_wide, caption_features_halfwidth.astype(jnp.float32), precision=lax.Precision.HIGHEST)
    caption_derivative = jnp.einsum('bgrs,bgrd->bgsd', coef_wide, picture_features_halfwidth.astype(jnp.float32), precision=lax.Precision.HIGHEST)
    return (per_line_penalty, picture_derivative, caption_derivative)

def project_back(unit, grad_unit, row_norm):
    return (grad_unit - unit * lax.optimization_barrier(jnp.sum(unit * grad_unit, -1, keepdims=True))) / row_norm

def reference(picture_features_unnormed, caption_features_unnormed, example_match_key, picture_loss_share, score_multiplier, score_shift):
    block_shape = (N_BLK, N_GROUP, ROWS, D)
    unit_img, img_norm = normalize(picture_features_unnormed)
    unit_txt, txt_norm = normalize(caption_features_unnormed)
    picture_features_halfwidth = unit_img.astype(jnp.bfloat16).reshape(block_shape)
    caption_features_halfwidth = unit_txt.astype(jnp.bfloat16).reshape(block_shape)
    match_keys_grouped = example_match_key.reshape(N_BLK, N_GROUP, ROWS)
    loss_shares = picture_loss_share.reshape(N_BLK, N_GROUP, ROWS)
    score_scaled_factor = score_multiplier[0]
    shifted_scores = score_shift[0]
    grad_unit_img = jnp.zeros(block_shape, jnp.float32)
    grad_unit_txt = jnp.zeros(block_shape, jnp.float32)
    row_total = jnp.zeros((N_BLK, N_GROUP, ROWS), jnp.float32)
    half_steps = STEPS // 2
    for offset in range(-(half_steps - 1), half_steps + 1):
        incoming_features = jnp.roll(caption_features_halfwidth, -offset, axis=0)
        incoming_match_keys = jnp.roll(match_keys_grouped, -offset, axis=0)
        per_line_penalty, picture_derivative, caption_derivative = match_contributions(picture_features_halfwidth, loss_shares, match_keys_grouped, incoming_features, incoming_match_keys, score_scaled_factor, shifted_scores)
        row_total = row_total + per_line_penalty
        grad_unit_img = grad_unit_img + picture_derivative
        grad_unit_txt = grad_unit_txt + jnp.roll(caption_derivative, offset, axis=0)
    loss_sum = jnp.sum(loss_shares * row_total)
    weight_sum = jnp.sum(loss_shares)
    loss = (loss_sum / weight_sum).reshape(1)
    image_grad = project_back(unit_img, grad_unit_img.reshape(BATCH, D), img_norm)
    text_grad = project_back(unit_txt, grad_unit_txt.reshape(BATCH, D), txt_norm)
    return (loss, image_grad, text_grad)
```

```python
import jax
import jax.numpy as jnp
from jax import lax
from jax.experimental import pallas as pl
from jax.experimental.pallas import tpu as pltpu
from jax.sharding import PartitionSpec as P

EXTRA = 16
CHUNK = 32
FAR = 2
VMEM_BYTES = 32 * 1024 * 1024


def from_ahead(value, axis, steps):
    count = lax.axis_size(axis)
    pairs = [((target + steps) % count, target) for target in range(count)]
    return lax.ppermute(value, axis, pairs)


def row_norms(values):
    return jnp.sqrt(jnp.sum(values * values, -1, keepdims=True) + 1e-06)


def vmem(count):
    return [pl.BlockSpec(memory_space=pltpu.VMEM)] * count


def call(kernel, outs, args, specs, scratch, flops, transcendentals, moved):
    return pl.pallas_call(
        kernel,
        out_shape=outs,
        in_specs=specs,
        out_specs=vmem(len(outs)),
        scratch_shapes=scratch,
        compiler_params=pltpu.CompilerParams(vmem_limit_bytes=VMEM_BYTES),
        cost_estimate=pl.CostEstimate(
            flops=flops, bytes_accessed=moved, transcendentals=transcendentals
        ),
    )(*args)


def prepare_kernel(img_ref, txt_ref, key_ref, weight_ref, pair_ref, img_out, txt_out):
    rows, width = img_ref.shape
    block = rows + EXTRA
    key = key_ref[...]
    weight = weight_ref[...]
    high = weight.astype(jnp.bfloat16).astype(jnp.float32)
    middle = (weight - high).astype(jnp.bfloat16).astype(jnp.float32)
    low = (weight - high) - middle
    line = lax.broadcasted_iota(jnp.int32, (EXTRA, width), 0)
    extra = jnp.zeros((EXTRA, width), jnp.float32)
    parts = (
        (key >> 8).astype(jnp.float32),
        (key & 255).astype(jnp.float32),
        high,
        middle,
        low,
    )
    for number, part in enumerate(parts):
        extra = jnp.where(line == number, part, extra)
    extra = extra.astype(jnp.bfloat16)
    for start, source, alone in ((0, img_ref, img_out), (block, txt_ref, txt_out)):
        values = source[...]
        unit = (values / row_norms(values)).astype(jnp.bfloat16)
        alone[0:rows, :] = unit
        alone[rows:block, :] = extra
        pair_ref[start : start + rows, :] = unit
        pair_ref[start + rows : start + block, :] = extra


def tile_kernel(
    scale_ref,
    shift_ref,
    weight_ref,
    pair_ref,
    img_ref,
    before_ref,
    own_ref,
    after_ref,
    sums_ref,
    pair_out,
    img_out,
    before_out,
    after_out,
    own_out,
    txts,
    imgs,
    scores,
    factors,
    columns,
):
    rows = own_ref.shape[0] - EXTRA
    width = own_ref.shape[1]
    block = rows + EXTRA
    scale = scale_ref[0]
    shift = shift_ref[0]

    imgs[0:rows, :] = pair_ref[0:rows, :]
    imgs[rows : 2 * rows, :] = img_ref[0:rows, :]
    txts[0:rows, :] = before_ref[0:rows, :]
    txts[rows : 2 * rows, :] = own_ref[0:rows, :]
    txts[2 * rows : 3 * rows, :] = after_ref[0:rows, :]
    txts[3 * rows : 4 * rows, :] = pair_ref[block : block + rows, :]

    lane = lax.broadcasted_iota(jnp.int32, (1, 4 * rows), 1)
    txt_keys = jnp.zeros((1, 4 * rows), jnp.float32)
    for slot, (source, start) in enumerate(
        ((before_ref, rows), (own_ref, rows), (after_ref, rows), (pair_ref, block + rows))
    ):
        extra = source[start : start + EXTRA, :].astype(jnp.float32)
        keys = extra[0:1] * 256.0 + extra[1:2]
        txt_keys = jnp.where(lane >= slot * rows, keys, txt_keys)

    one = lax.broadcasted_iota(jnp.int32, (rows, 256), 0) == lax.broadcasted_iota(
        jnp.int32, (rows, 256), 1
    )
    one = jnp.where(one, 1.0, 0.0).astype(jnp.bfloat16)
    for slot, source in enumerate((pair_ref, img_ref)):
        columns[slot * rows : (slot + 1) * rows, :] = lax.dot_general(
            one,
            source[rows : rows + EXTRA, 0:256],
            (((1,), (1,)), ((), ())),
            preferred_element_type=jnp.float32,
        )

    scores[...] = lax.dot_general(
        imgs[...], txts[...], (((1,), (1,)), ((), ())), preferred_element_type=jnp.float32
    )

    def step(number, total):
        here = pl.ds(pl.multiple_of(number * CHUNK, CHUNK), CHUNK)
        column = columns[here, :]
        img_keys = column[:, 0:1] * 256.0 + column[:, 1:2]
        weights = (column[:, 2:3] + column[:, 3:4]) + column[:, 4:5]
        same = img_keys == txt_keys
        score = scale * scores[here, :] + shift
        argument = jnp.where(same, -score, score)
        small = jnp.exp(-jnp.abs(argument))
        penalty = jnp.maximum(argument, 0.0) + jnp.log1p(small)
        share = 1.0 / (1.0 + small)
        sigmoid = jnp.where(argument >= 0.0, share, small * share)
        scaled = weights * scale
        factors[here, :] = (jnp.where(same, -scaled, scaled) * sigmoid).astype(jnp.bfloat16)
        return total + weights * penalty

    total = lax.fori_loop(
        0, 2 * rows // CHUNK, step, jnp.zeros((CHUNK, 4 * rows), jnp.float32)
    )
    loss_part = jnp.sum(jnp.sum(total, 0, keepdims=True), 1, keepdims=True)
    weight_part = jnp.sum(weight_ref[...], 1, keepdims=True)
    place = lax.broadcasted_iota(jnp.int32, sums_ref.shape, 1)
    sums_ref[...] = jnp.where(
        place == 0, loss_part, jnp.where(place == 1, weight_part, 0.0)
    )

    img_grads = jnp.dot(factors[...], txts[...], preferred_element_type=jnp.float32)
    img_grads = img_grads.astype(jnp.bfloat16)
    pair_out[0:rows, :] = img_grads[0:rows]
    img_out[...] = img_grads[rows : 2 * rows]
    txt_grads = lax.dot_general(
        factors[...], imgs[...], (((0,), (0,)), ((), ())), preferred_element_type=jnp.float32
    )
    before_out[...] = txt_grads[0:rows].astype(jnp.bfloat16)
    own_out[...] = txt_grads[rows : 2 * rows]
    after_out[...] = txt_grads[2 * rows : 3 * rows].astype(jnp.bfloat16)
    pair_out[rows : 2 * rows, :] = txt_grads[3 * rows : 4 * rows].astype(jnp.bfloat16)


def finish_kernel(
    img_ref, txt_ref, pair_ref, far_ref, after_ref, before_ref, own_ref, img_out, txt_out
):
    rows = img_ref.shape[0]

    def finish(values, grad):
        norm = row_norms(values)
        unit = values / norm
        return (grad - unit * jnp.sum(unit * grad, -1, keepdims=True)) / norm

    wide = lambda part: part.astype(jnp.float32)
    img_out[...] = finish(img_ref[...], wide(pair_ref[0:rows, :]) + wide(far_ref[...]))
    txt_out[...] = finish(
        txt_ref[...],
        (own_ref[...] + wide(before_ref[...]))
        + (wide(after_ref[...]) + wide(pair_ref[rows : 2 * rows, :])),
    )


def sum_over(part, axis):
    count = lax.axis_size(axis)
    spread = jnp.broadcast_to(part, (count, part.shape[-1]))
    gathered = lax.all_to_all(spread, axis, 0, 0, tiled=True)
    return jnp.sum(gathered, 0, keepdims=True)


def per_device(image_emb, text_emb, keys, weights, scale, shift):
    rows, width = image_emb.shape
    block = rows + EXTRA
    half = lambda *shape: jax.ShapeDtypeStruct(shape, jnp.bfloat16)
    full = lambda *shape: jax.ShapeDtypeStruct(shape, jnp.float32)
    repeats = width // rows
    wide_keys = jnp.tile(keys, repeats).reshape(1, width)
    wide_weights = jnp.tile(weights, repeats).reshape(1, width)
    pair, img_block, txt_block = call(
        prepare_kernel,
        [half(2 * block, width), half(block, width), half(block, width)],
        (image_emb, text_emb, wide_keys, wide_weights),
        vmem(4),
        [],
        6 * rows * width,
        0,
        16 * rows * width,
    )
    pair_ahead = from_ahead(pair, "blk", FAR)
    img_behind = from_ahead(img_block, "blk", -FAR)
    txt_after = from_ahead(txt_block, "blk", 1)
    txt_before = from_ahead(txt_block, "blk", -1)
    sums, pair_part, img_part, before_part, after_part, own_part = call(
        tile_kernel,
        [
            full(8, 128),
            half(2 * rows, width),
            half(rows, width),
            half(rows, width),
            half(rows, width),
            full(rows, width),
        ],
        (
            scale,
            shift,
            weights.reshape(1, rows),
            pair_ahead,
            img_behind,
            txt_before,
            txt_block,
            txt_after,
        ),
        [pl.BlockSpec(memory_space=pltpu.SMEM)] * 2 + vmem(6),
        [
            pltpu.VMEM((4 * rows, width), jnp.bfloat16),
            pltpu.VMEM((2 * rows, width), jnp.bfloat16),
            pltpu.VMEM((2 * rows, 4 * rows), jnp.float32),
            pltpu.VMEM((2 * rows, 4 * rows), jnp.bfloat16),
            pltpu.VMEM((2 * rows, EXTRA), jnp.float32),
        ],
        48 * rows * rows * width,
        24 * rows * rows,
        28 * rows * width,
    )
    pair_back = from_ahead(pair_part, "blk", -FAR)
    far_back = from_ahead(img_part, "blk", FAR)
    after_back = from_ahead(before_part, "blk", 1)
    before_back = from_ahead(after_part, "blk", -1)
    image_grad, text_grad = call(
        finish_kernel,
        [full(rows, width), full(rows, width)],
        (
            image_emb,
            text_emb,
            pair_back,
            far_back,
            after_back,
            before_back,
            own_part,
        ),
        vmem(7),
        [],
        20 * rows * width,
        0,
        30 * rows * width,
    )
    sums = sum_over(sum_over(sums[0:1], "blk"), "group")
    loss = sums[0, 0:1] / sums[0, 1:2]
    return (loss, image_grad, text_grad)


def solution(mesh):
    split = ("blk", "group")
    placed = (P(split, None), P(split, None), P(split), P(split), P(), P())
    return jax.shard_map(
        per_device,
        mesh=mesh,
        in_specs=placed,
        out_specs=(P(), P(split, None), P(split, None)),
        check_vma=False,
    )
```

```python
import jax
import jax.numpy as jnp
from jax import lax
from jax.experimental import pallas as pl
from jax.experimental.pallas import tpu as pltpu
from jax.sharding import PartitionSpec as P

EXTRA = 16
CHUNK = 32
FAR = 2
VMEM_BYTES = 16 * 1024 * 1024
PLANE = 8
Z_HI = 4


def from_ahead(value, axis, steps):
    count = lax.axis_size(axis)
    pairs = [((target + steps) % count, target) for target in range(count)]
    return lax.ppermute(value, axis, pairs)


def row_norms(values):
    return jnp.sqrt(jnp.sum(values * values, -1, keepdims=True) + 1e-06)


def vmem(count):
    return [pl.BlockSpec(memory_space=pltpu.VMEM)] * count


def call(kernel, outs, args, specs, scratch, flops, transcendentals, moved, limit):
    return pl.pallas_call(
        kernel,
        out_shape=outs,
        in_specs=specs,
        out_specs=vmem(len(outs)),
        scratch_shapes=scratch,
        compiler_params=pltpu.CompilerParams(vmem_limit_bytes=limit),
        cost_estimate=pl.CostEstimate(
            flops=flops, bytes_accessed=moved, transcendentals=transcendentals
        ),
    )(*args)


def prepare_kernel(
    img_ref, txt_ref, key_ref, weight_ref, pair_ref, txt_out, img_out, again_out, img_buf, txt_buf, sems
):
    rows, width = img_buf.shape
    block = rows + EXTRA
    copies = [
        pltpu.make_async_copy(source, target, sems.at[number])
        for number, (source, target) in enumerate(((img_ref, img_buf), (txt_ref, txt_buf)))
    ]
    for copy in copies:
        copy.start()
    key = key_ref[...]
    weight = weight_ref[...]
    high = weight.astype(jnp.bfloat16).astype(jnp.float32)
    middle = (weight - high).astype(jnp.bfloat16).astype(jnp.float32)
    low = (weight - high) - middle
    line = lax.broadcasted_iota(jnp.int32, (EXTRA, rows), 0)
    extra = jnp.zeros((EXTRA, rows), jnp.float32)
    parts = (
        (key >> 8).astype(jnp.float32),
        (key & 255).astype(jnp.float32),
        high,
        middle,
        low,
    )
    for number, part in enumerate(parts):
        extra = jnp.where(line == number, part, extra)
    place = lax.broadcasted_iota(jnp.int32, (rows, width), 1) - lax.broadcasted_iota(
        jnp.int32, (rows, width), 0
    )
    hit = place == 0
    for number in range(1, width // rows):
        hit = jnp.logical_or(hit, place == number * rows)
    extra = jnp.dot(
        extra.astype(jnp.bfloat16),
        jnp.where(hit, 1.0, 0.0).astype(jnp.bfloat16),
        preferred_element_type=jnp.float32,
    ).astype(jnp.bfloat16)
    for start, source, alone, copy in (
        (0, img_buf, (img_out,), copies[0]),
        (block, txt_buf, (txt_out, again_out), copies[1]),
    ):
        copy.wait()
        values = source[...]
        unit = (values / row_norms(values)).astype(jnp.bfloat16)
        for target in (*alone, pair_ref.at[start : start + block]):
            target[0:rows, :] = unit
            target[rows:block, :] = extra


def stack_blocks(rows, pair_ref, after_ref, img_ref, before_ref, own_ref, txts, imgs):
    block = rows + EXTRA
    imgs[0:rows, :] = pair_ref[0:rows, :]
    imgs[rows : 2 * rows, :] = img_ref[0:rows, :]
    txts[0:rows, :] = before_ref[0:rows, :]
    txts[rows : 2 * rows, :] = own_ref[0:rows, :]
    txts[2 * rows : 3 * rows, :] = after_ref[0:rows, :]
    txts[3 * rows : 4 * rows, :] = pair_ref[block : block + rows, :]


def score_kernel(
    scale_ref,
    shift_ref,
    weight_ref,
    pair_ref,
    after_ref,
    img_ref,
    before_ref,
    own_ref,
    sums_ref,
    factors,
    txts,
    imgs,
    scores,
    columns,
):
    rows = own_ref.shape[0] - EXTRA
    block = rows + EXTRA
    scale = scale_ref[0]
    shift = shift_ref[0]

    stack_blocks(rows, pair_ref, after_ref, img_ref, before_ref, own_ref, txts, imgs)

    lane = lax.broadcasted_iota(jnp.int32, (1, 4 * rows), 1)
    txt_keys = jnp.zeros((1, 4 * rows), jnp.float32)
    for slot, (source, start) in enumerate(
        ((before_ref, rows), (own_ref, rows), (after_ref, rows), (pair_ref, block + rows))
    ):
        extra = source[start : start + EXTRA, :].astype(jnp.float32)
        keys = extra[0:1] * 256.0 + extra[1:2]
        txt_keys = jnp.where(lane >= slot * rows, keys, txt_keys)

    one = lax.broadcasted_iota(jnp.int32, (rows, 256), 0) == lax.broadcasted_iota(
        jnp.int32, (rows, 256), 1
    )
    one = jnp.where(one, 1.0, 0.0).astype(jnp.bfloat16)
    for slot, source in enumerate((pair_ref, img_ref)):
        columns[slot * rows : (slot + 1) * rows, :] = lax.dot_general(
            one,
            source[rows : rows + EXTRA, 0:256],
            (((1,), (1,)), ((), ())),
            preferred_element_type=jnp.float32,
        )

    scores[...] = lax.dot_general(
        imgs[...], txts[...], (((1,), (1,)), ((), ())), preferred_element_type=jnp.float32
    )

    def step(number, total):
        here = pl.ds(pl.multiple_of(number * CHUNK, CHUNK), CHUNK)
        column = columns[here, :]
        img_keys = column[:, 0:1] * 256.0 + column[:, 1:2]
        weights = (column[:, 2:3] + column[:, 3:4]) + column[:, 4:5]
        same = img_keys == txt_keys
        score = scale * scores[here, :] + shift
        argument = jnp.where(same, -score, score)
        small = jnp.exp(-jnp.abs(argument))
        penalty = jnp.maximum(argument, 0.0) + jnp.log1p(small)
        share = 1.0 / (1.0 + small)
        sigmoid = jnp.where(argument >= 0.0, share, small * share)
        scaled = weights * scale
        factors[here, :] = (jnp.where(same, -scaled, scaled) * sigmoid).astype(jnp.bfloat16)
        return total + weights * penalty

    total = lax.fori_loop(
        0, 2 * rows // CHUNK, step, jnp.zeros((CHUNK, 4 * rows), jnp.float32)
    )
    loss_part = jnp.sum(jnp.sum(total, 0, keepdims=True), 1, keepdims=True)
    weight_part = jnp.sum(weight_ref[...], 1, keepdims=True)
    place = lax.broadcasted_iota(jnp.int32, sums_ref.shape, 1)
    sums_ref[...] = jnp.where(
        place == 0, loss_part, jnp.where(place == 1, weight_part, 0.0)
    )


def grad_kernel(
    factors,
    pair_ref,
    after_ref,
    img_ref,
    before_ref,
    own_ref,
    pair_out,
    img_out,
    before_out,
    after_out,
    own_out,
    txts,
    imgs,
):
    rows = own_out.shape[0]
    stack_blocks(rows, pair_ref, after_ref, img_ref, before_ref, own_ref, txts, imgs)
    img_grads = jnp.dot(factors[...], txts[...], preferred_element_type=jnp.float32)
    img_grads = img_grads.astype(jnp.bfloat16)
    pair_out[0:rows, :] = img_grads[0:rows]
    img_out[...] = img_grads[rows : 2 * rows]
    txt_grads = lax.dot_general(
        factors[...], imgs[...], (((0,), (0,)), ((), ())), preferred_element_type=jnp.float32
    )
    before_out[...] = txt_grads[0:rows].astype(jnp.bfloat16)
    own_out[...] = txt_grads[rows : 2 * rows]
    after_out[...] = txt_grads[2 * rows : 3 * rows].astype(jnp.bfloat16)
    pair_out[rows : 2 * rows, :] = txt_grads[3 * rows : 4 * rows].astype(jnp.bfloat16)


def finish_kernel(
    img_ref, txt_ref, pair_ref, before_ref, far_ref, after_ref, own_ref, sums_ref,
    img_out, txt_out, loss_out
):
    rows = img_ref.shape[0]

    def finish(values, grad):
        norm = row_norms(values)
        unit = values / norm
        return (grad - unit * jnp.sum(unit * grad, -1, keepdims=True)) / norm

    wide = lambda part: part.astype(jnp.float32)
    img_out[...] = finish(img_ref[...], wide(pair_ref[0:rows, :]) + wide(far_ref[...]))
    txt_out[...] = finish(
        txt_ref[...],
        (own_ref[...] + wide(before_ref[...]))
        + (wide(after_ref[...]) + wide(pair_ref[rows : 2 * rows, :])),
    )
    sums = jnp.sum(sums_ref[...], 0, keepdims=True)
    loss_out[...] = sums[:, 0:1] / sums[:, 1:2]


def exchange(part, groups):
    count = len(groups[0])
    spread = jnp.broadcast_to(part.reshape(1, 1, -1), (count, 1, part.shape[-1]))
    return lax.all_to_all(
        spread, ("blk", "group"), 0, 0, tiled=True, axis_index_groups=groups
    ).reshape(count, -1)


def plane_and_column_groups():
    blk, group = lax.axis_size("blk"), lax.axis_size("group")
    planes, columns = {}, {}
    for number in range(blk * group):
        first, second = number // group, number % group
        z = (second % Z_HI, first // PLANE)
        planes.setdefault(z, []).append(number)
        columns.setdefault((first % PLANE, second // Z_HI), []).append(number)
    return list(planes.values()), list(columns.values())


def per_device(image_emb, text_emb, keys, weights, scale, shift):
    rows, width = image_emb.shape
    block = rows + EXTRA
    half = lambda *shape: jax.ShapeDtypeStruct(shape, jnp.bfloat16)
    full = lambda *shape: jax.ShapeDtypeStruct(shape, jnp.float32)
    smem = [pl.BlockSpec(memory_space=pltpu.SMEM)] * 2
    hbm = [pl.BlockSpec(memory_space=pltpu.HBM)] * 2
    row_weights = weights.reshape(1, rows)
    fixed = [pltpu.with_memory_space_constraint(x, pltpu.HBM) for x in (image_emb, text_emb)]
    pair, txt_block, img_block, txt_again = call(
        prepare_kernel,
        [half(2 * block, width)] + [half(block, width)] * 3,
        (*fixed, keys.reshape(1, rows), row_weights),
        hbm + vmem(2),
        [
            pltpu.VMEM((rows, width), jnp.float32),
            pltpu.VMEM((rows, width), jnp.float32),
            pltpu.SemaphoreType.DMA((2,)),
        ],
        6 * rows * width,
        0,
        16 * rows * width,
        VMEM_BYTES,
    )
    pair_ahead = from_ahead(pair, "blk", FAR)
    txt_after = from_ahead(txt_block, "blk", 1)
    img_behind = from_ahead(img_block, "blk", -FAR)
    txt_before = from_ahead(txt_again, "blk", -1)
    blocks = (pair_ahead, txt_after, img_behind, txt_before, txt_block)
    stacks = [
        pltpu.VMEM((4 * rows, width), jnp.bfloat16),
        pltpu.VMEM((2 * rows, width), jnp.bfloat16),
    ]
    sums, factors = call(
        score_kernel,
        [full(8, 128), half(2 * rows, 4 * rows)],
        (scale, shift, row_weights, *blocks),
        smem + vmem(6),
        stacks
        + [
            pltpu.VMEM((2 * rows, 4 * rows), jnp.float32),
            pltpu.VMEM((2 * rows, EXTRA), jnp.float32),
        ],
        16 * rows * rows * width,
        24 * rows * rows,
        28 * rows * width,
        VMEM_BYTES,
    )
    parts = call(
        grad_kernel,
        [
            half(2 * rows, width),
            half(rows, width),
            half(rows, width),
            half(rows, width),
            full(rows, width),
        ],
        (factors, *blocks),
        vmem(6),
        stacks,
        32 * rows * rows * width,
        0,
        28 * rows * width,
        VMEM_BYTES,
    )
    planes, columns = plane_and_column_groups()
    gathered = exchange(sums[0:1], planes)
    pair_part, img_part, before_part, after_part, own_part = parts
    pair_back = from_ahead(pair_part, "blk", -FAR)
    before_back = from_ahead(after_part, "blk", -1)
    far_back = from_ahead(img_part, "blk", FAR)
    after_back = from_ahead(before_part, "blk", 1)
    gathered = exchange(jnp.sum(gathered, 0, keepdims=True), columns)
    image_grad, text_grad, loss = call(
        finish_kernel,
        [full(rows, width), full(rows, width), full(1, 1)],
        (
            image_emb,
            text_emb,
            pair_back,
            before_back,
            far_back,
            after_back,
            own_part,
            gathered,
        ),
        vmem(8),
        [],
        20 * rows * width,
        0,
        30 * rows * width,
        VMEM_BYTES,
    )
    return (loss.reshape(1), image_grad, text_grad)


def solution(mesh):
    split = ("blk", "group")
    placed = (P(split, None), P(split, None), P(split), P(split), P(), P())
    return jax.shard_map(
        per_device,
        mesh=mesh,
        in_specs=placed,
        out_specs=(P(), P(split, None), P(split, None)),
        check_vma=False,
    )
```

```python
import jax
import jax.numpy as jnp
from jax import lax
from jax.experimental import pallas as pl
from jax.experimental.pallas import tpu as pltpu
from jax.sharding import PartitionSpec as P

EXTRA = 16
CHUNK = 32
FAR = 2
VMEM_BYTES = 16 * 1024 * 1024
PLANE = 8
Z_HI = 4


def from_ahead(value, axis, steps):
    count = lax.axis_size(axis)
    pairs = [((target + steps) % count, target) for target in range(count)]
    return lax.ppermute(value, axis, pairs)


def row_norms(values):
    return jnp.sqrt(jnp.sum(values * values, -1, keepdims=True) + 1e-06)


def vmem(count):
    return [pl.BlockSpec(memory_space=pltpu.VMEM)] * count


def call(kernel, outs, args, specs, scratch, flops, transcendentals, moved, limit):
    return pl.pallas_call(
        kernel,
        out_shape=outs,
        in_specs=specs,
        out_specs=vmem(len(outs)),
        scratch_shapes=scratch,
        compiler_params=pltpu.CompilerParams(vmem_limit_bytes=limit),
        cost_estimate=pl.CostEstimate(
            flops=flops, bytes_accessed=moved, transcendentals=transcendentals
        ),
    )(*args)


def prepare_kernel(
    img_ref, txt_ref, key_ref, weight_ref, pair_ref, txt_out, img_out, again_out, img_buf, txt_buf, sems
):
    rows, width = img_buf.shape
    block = rows + EXTRA
    copies = [
        pltpu.make_async_copy(source, target, sems.at[number])
        for number, (source, target) in enumerate(((img_ref, img_buf), (txt_ref, txt_buf)))
    ]
    for copy in copies:
        copy.start()
    key = key_ref[...]
    weight = weight_ref[...]
    high = weight.astype(jnp.bfloat16).astype(jnp.float32)
    middle = (weight - high).astype(jnp.bfloat16).astype(jnp.float32)
    low = (weight - high) - middle
    line = lax.broadcasted_iota(jnp.int32, (EXTRA, rows), 0)
    extra = jnp.zeros((EXTRA, rows), jnp.float32)
    parts = (
        (key >> 8).astype(jnp.float32),
        (key & 255).astype(jnp.float32),
        high,
        middle,
        low,
    )
    for number, part in enumerate(parts):
        extra = jnp.where(line == number, part, extra)
    place = lax.broadcasted_iota(jnp.int32, (rows, width), 1) - lax.broadcasted_iota(
        jnp.int32, (rows, width), 0
    )
    hit = place == 0
    for number in range(1, width // rows):
        hit = jnp.logical_or(hit, place == number * rows)
    extra = jnp.dot(
        extra.astype(jnp.bfloat16),
        jnp.where(hit, 1.0, 0.0).astype(jnp.bfloat16),
        preferred_element_type=jnp.float32,
    ).astype(jnp.bfloat16)
    for start, source, alone, copy in (
        (0, img_buf, (img_out,), copies[0]),
        (block, txt_buf, (txt_out, again_out), copies[1]),
    ):
        copy.wait()
        values = source[...]
        unit = (values / row_norms(values)).astype(jnp.bfloat16)
        for target in (*alone, pair_ref.at[start : start + block]):
            target[0:rows, :] = unit
            target[rows:block, :] = extra


def stack_blocks(rows, pair_ref, after_ref, img_ref, before_ref, own_ref, txts, imgs):
    block = rows + EXTRA
    imgs[0:rows, :] = pair_ref[0:rows, :]
    imgs[rows : 2 * rows, :] = img_ref[0:rows, :]
    txts[0:rows, :] = before_ref[0:rows, :]
    txts[rows : 2 * rows, :] = own_ref[0:rows, :]
    txts[2 * rows : 3 * rows, :] = after_ref[0:rows, :]
    txts[3 * rows : 4 * rows, :] = pair_ref[block : block + rows, :]


def score_kernel(
    scale_ref,
    shift_ref,
    weight_ref,
    pair_ref,
    after_ref,
    img_ref,
    before_ref,
    own_ref,
    sums_ref,
    factors,
    txts,
    imgs,
    scores,
    columns,
):
    rows = own_ref.shape[0] - EXTRA
    block = rows + EXTRA
    scale = scale_ref[0]
    shift = shift_ref[0]

    stack_blocks(rows, pair_ref, after_ref, img_ref, before_ref, own_ref, txts, imgs)

    lane = lax.broadcasted_iota(jnp.int32, (1, 4 * rows), 1)
    txt_keys = jnp.zeros((1, 4 * rows), jnp.float32)
    for slot, (source, start) in enumerate(
        ((before_ref, rows), (own_ref, rows), (after_ref, rows), (pair_ref, block + rows))
    ):
        extra = source[start : start + EXTRA, :].astype(jnp.float32)
        keys = extra[0:1] * 256.0 + extra[1:2]
        txt_keys = jnp.where(lane >= slot * rows, keys, txt_keys)

    one = lax.broadcasted_iota(jnp.int32, (rows, 256), 0) == lax.broadcasted_iota(
        jnp.int32, (rows, 256), 1
    )
    one = jnp.where(one, 1.0, 0.0).astype(jnp.bfloat16)
    for slot, source in enumerate((pair_ref, img_ref)):
        columns[slot * rows : (slot + 1) * rows, :] = lax.dot_general(
            one,
            source[rows : rows + EXTRA, 0:256],
            (((1,), (1,)), ((), ())),
            preferred_element_type=jnp.float32,
        )

    scores[...] = lax.dot_general(
        imgs[...], txts[...], (((1,), (1,)), ((), ())), preferred_element_type=jnp.float32
    )

    def step(number, total):
        here = pl.ds(pl.multiple_of(number * CHUNK, CHUNK), CHUNK)
        column = columns[here, :]
        img_keys = column[:, 0:1] * 256.0 + column[:, 1:2]
        weights = (column[:, 2:3] + column[:, 3:4]) + column[:, 4:5]
        same = img_keys == txt_keys
        score = scale * scores[here, :] + shift
        argument = jnp.where(same, -score, score)
        small = jnp.exp(-jnp.abs(argument))
        penalty = jnp.maximum(argument, 0.0) + jnp.log1p(small)
        share = 1.0 / (1.0 + small)
        sigmoid = jnp.where(argument >= 0.0, share, small * share)
        scaled = weights * scale
        factors[here, :] = (jnp.where(same, -scaled, scaled) * sigmoid).astype(jnp.bfloat16)
        return total + weights * penalty

    total = lax.fori_loop(
        0, 2 * rows // CHUNK, step, jnp.zeros((CHUNK, 4 * rows), jnp.float32)
    )
    loss_part = jnp.sum(jnp.sum(total, 0, keepdims=True), 1, keepdims=True)
    weight_part = jnp.sum(weight_ref[...], 1, keepdims=True)
    place = lax.broadcasted_iota(jnp.int32, sums_ref.shape, 1)
    sums_ref[...] = jnp.where(
        place == 0, loss_part, jnp.where(place == 1, weight_part, 0.0)
    )


def grad_kernel(
    factors,
    pair_ref,
    after_ref,
    img_ref,
    before_ref,
    own_ref,
    pair_out,
    img_out,
    before_out,
    after_out,
    own_out,
    txts,
    imgs,
):
    rows = own_out.shape[0]
    stack_blocks(rows, pair_ref, after_ref, img_ref, before_ref, own_ref, txts, imgs)
    img_grads = jnp.dot(factors[...], txts[...], preferred_element_type=jnp.float32)
    img_grads = img_grads.astype(jnp.bfloat16)
    pair_out[0:rows, :] = img_grads[0:rows]
    img_out[...] = img_grads[rows : 2 * rows]
    txt_grads = lax.dot_general(
        factors[...], imgs[...], (((0,), (0,)), ((), ())), preferred_element_type=jnp.float32
    )
    before_out[...] = txt_grads[0:rows].astype(jnp.bfloat16)
    own_out[...] = txt_grads[rows : 2 * rows]
    after_out[...] = txt_grads[2 * rows : 3 * rows].astype(jnp.bfloat16)
    pair_out[rows : 2 * rows, :] = txt_grads[3 * rows : 4 * rows].astype(jnp.bfloat16)


def finish_kernel(
    img_ref, txt_ref, pair_ref, before_ref, far_ref, after_ref, own_ref, sums_ref,
    img_out, txt_out, loss_out
):
    rows = img_ref.shape[0]

    def finish(values, grad):
        norm = row_norms(values)
        unit = values / norm
        return (grad - unit * jnp.sum(unit * grad, -1, keepdims=True)) / norm

    wide = lambda part: part.astype(jnp.float32)
    img_out[...] = finish(img_ref[...], wide(pair_ref[0:rows, :]) + wide(far_ref[...]))
    txt_out[...] = finish(
        txt_ref[...],
        (own_ref[...] + wide(before_ref[...]))
        + (wide(after_ref[...]) + wide(pair_ref[rows : 2 * rows, :])),
    )
    sums = jnp.sum(sums_ref[...], 0, keepdims=True)
    loss_out[...] = sums[:, 0:1] / sums[:, 1:2]


def exchange(part, groups):
    count = len(groups[0])
    spread = jnp.broadcast_to(part.reshape(1, 1, -1), (count, 1, part.shape[-1]))
    return lax.all_to_all(
        spread, ("blk", "group"), 0, 0, tiled=True, axis_index_groups=groups
    ).reshape(count, -1)


def plane_and_column_groups():
    blk, group = lax.axis_size("blk"), lax.axis_size("group")
    planes, columns = {}, {}
    for number in range(blk * group):
        first, second = number // group, number % group
        z = (second % Z_HI, first // PLANE)
        planes.setdefault(z, []).append(number)
        columns.setdefault((first % PLANE, second // Z_HI), []).append(number)
    return list(planes.values()), list(columns.values())


def per_device(image_emb, text_emb, keys, weights, scale, shift):
    rows, width = image_emb.shape
    block = rows + EXTRA
    half = lambda *shape: jax.ShapeDtypeStruct(shape, jnp.bfloat16)
    full = lambda *shape: jax.ShapeDtypeStruct(shape, jnp.float32)
    smem = [pl.BlockSpec(memory_space=pltpu.SMEM)] * 2
    hbm = [pl.BlockSpec(memory_space=pltpu.HBM)] * 2
    row_weights = weights.reshape(1, rows)
    fixed = [pltpu.with_memory_space_constraint(x, pltpu.HBM) for x in (image_emb, text_emb)]
    pair, txt_block, img_block, txt_again = call(
        prepare_kernel,
        [half(2 * block, width)] + [half(block, width)] * 3,
        (*fixed, keys.reshape(1, rows), row_weights),
        hbm + vmem(2),
        [
            pltpu.VMEM((rows, width), jnp.float32),
            pltpu.VMEM((rows, width), jnp.float32),
            pltpu.SemaphoreType.DMA((2,)),
        ],
        6 * rows * width,
        0,
        16 * rows * width,
        VMEM_BYTES,
    )
    pair_ahead = from_ahead(pair, "blk", FAR)
    txt_after = from_ahead(txt_again, "blk", 1)
    img_behind = from_ahead(img_block, "blk", -FAR)
    txt_before = from_ahead(txt_block, "blk", -1)
    blocks = (pair_ahead, txt_after, img_behind, txt_before, txt_block)
    stacks = [
        pltpu.VMEM((4 * rows, width), jnp.bfloat16),
        pltpu.VMEM((2 * rows, width), jnp.bfloat16),
    ]
    sums, factors = call(
        score_kernel,
        [full(8, 128), half(2 * rows, 4 * rows)],
        (scale, shift, row_weights, *blocks),
        smem + vmem(6),
        stacks
        + [
            pltpu.VMEM((2 * rows, 4 * rows), jnp.float32),
            pltpu.VMEM((2 * rows, EXTRA), jnp.float32),
        ],
        16 * rows * rows * width,
        24 * rows * rows,
        28 * rows * width,
        VMEM_BYTES,
    )
    parts = call(
        grad_kernel,
        [
            half(2 * rows, width),
            half(rows, width),
            half(rows, width),
            half(rows, width),
            full(rows, width),
        ],
        (factors, *blocks),
        vmem(6),
        stacks,
        32 * rows * rows * width,
        0,
        28 * rows * width,
        VMEM_BYTES,
    )
    planes, columns = plane_and_column_groups()
    gathered = exchange(sums[0:1], planes)
    pair_part, img_part, before_part, after_part, own_part = parts
    pair_back = from_ahead(pair_part, "blk", -FAR)
    before_back = from_ahead(after_part, "blk", -1)
    far_back = from_ahead(img_part, "blk", FAR)
    after_back = from_ahead(before_part, "blk", 1)
    gathered = exchange(jnp.sum(gathered, 0, keepdims=True), columns)
    image_grad, text_grad, loss = call(
        finish_kernel,
        [full(rows, width), full(rows, width), full(1, 1)],
        (
            image_emb,
            text_emb,
            pair_back,
            before_back,
            far_back,
            after_back,
            own_part,
            gathered,
        ),
        vmem(8),
        [],
        20 * rows * width,
        0,
        30 * rows * width,
        VMEM_BYTES,
    )
    return (loss.reshape(1), image_grad, text_grad)


def solution(mesh):
    split = ("blk", "group")
    placed = (P(split, None), P(split, None), P(split), P(split), P(), P())
    return jax.shard_map(
        per_device,
        mesh=mesh,
        in_specs=placed,
        out_specs=(P(), P(split, None), P(split, None)),
        check_vma=False,
    )
```

```python
import jax
import jax.numpy as jnp
from jax import lax
from jax.experimental import pallas as pl
from jax.experimental.pallas import tpu as pltpu
from jax.sharding import PartitionSpec as P

EXTRA = 16
CHUNK = 32
FAR = 2
VMEM_BYTES = 16 * 1024 * 1024
PLANE = 8
Z_HI = 4


def from_ahead(value, axis, steps):
    count = lax.axis_size(axis)
    pairs = [((target + steps) % count, target) for target in range(count)]
    return lax.ppermute(value, axis, pairs)


def row_norms(values):
    return jnp.sqrt(jnp.sum(values * values, -1, keepdims=True) + 1e-06)


def vmem(count):
    return [pl.BlockSpec(memory_space=pltpu.VMEM)] * count


def call(kernel, outs, args, specs, scratch, flops, transcendentals, moved, limit):
    return pl.pallas_call(
        kernel,
        out_shape=outs,
        in_specs=specs,
        out_specs=vmem(len(outs)),
        scratch_shapes=scratch,
        compiler_params=pltpu.CompilerParams(vmem_limit_bytes=limit),
        cost_estimate=pl.CostEstimate(
            flops=flops, bytes_accessed=moved, transcendentals=transcendentals
        ),
    )(*args)


def prepare_kernel(
    img_ref, txt_ref, key_ref, weight_ref, pair_ref, txt_out, img_out, again_out, img_buf, txt_buf, sems
):
    rows, width = img_buf.shape
    block = rows + EXTRA
    copies = [
        pltpu.make_async_copy(source, target, sems.at[number])
        for number, (source, target) in enumerate(((img_ref, img_buf), (txt_ref, txt_buf)))
    ]
    for copy in copies:
        copy.start()
    key = key_ref[...]
    weight = weight_ref[...]
    high = weight.astype(jnp.bfloat16).astype(jnp.float32)
    middle = (weight - high).astype(jnp.bfloat16).astype(jnp.float32)
    low = (weight - high) - middle
    line = lax.broadcasted_iota(jnp.int32, (EXTRA, rows), 0)
    extra = jnp.zeros((EXTRA, rows), jnp.float32)
    parts = (
        (key >> 8).astype(jnp.float32),
        (key & 255).astype(jnp.float32),
        high,
        middle,
        low,
    )
    for number, part in enumerate(parts):
        extra = jnp.where(line == number, part, extra)
    place = lax.broadcasted_iota(jnp.int32, (rows, width), 1) - lax.broadcasted_iota(
        jnp.int32, (rows, width), 0
    )
    hit = place == 0
    for number in range(1, width // rows):
        hit = jnp.logical_or(hit, place == number * rows)
    extra = jnp.dot(
        extra.astype(jnp.bfloat16),
        jnp.where(hit, 1.0, 0.0).astype(jnp.bfloat16),
        preferred_element_type=jnp.float32,
    ).astype(jnp.bfloat16)
    for start, source, alone, copy in (
        (0, img_buf, (img_out,), copies[0]),
        (block, txt_buf, (txt_out, again_out), copies[1]),
    ):
        copy.wait()
        values = source[...]
        unit = (values / row_norms(values)).astype(jnp.bfloat16)
        for target in (*alone, pair_ref.at[start : start + block]):
            target[0:rows, :] = unit
            target[rows:block, :] = extra


def stack_blocks(rows, pair_ref, after_ref, img_ref, before_ref, own_ref, txts, imgs):
    block = rows + EXTRA
    imgs[0:rows, :] = pair_ref[0:rows, :]
    imgs[rows : 2 * rows, :] = img_ref[0:rows, :]
    txts[0:rows, :] = before_ref[0:rows, :]
    txts[rows : 2 * rows, :] = own_ref[0:rows, :]
    txts[2 * rows : 3 * rows, :] = after_ref[0:rows, :]
    txts[3 * rows : 4 * rows, :] = pair_ref[block : block + rows, :]


def score_kernel(
    scale_ref,
    shift_ref,
    weight_ref,
    pair_ref,
    after_ref,
    img_ref,
    before_ref,
    own_ref,
    sums_ref,
    factors,
    txts,
    imgs,
    scores,
    columns,
):
    rows = own_ref.shape[0] - EXTRA
    block = rows + EXTRA
    scale = scale_ref[0]
    shift = shift_ref[0]

    stack_blocks(rows, pair_ref, after_ref, img_ref, before_ref, own_ref, txts, imgs)

    lane = lax.broadcasted_iota(jnp.int32, (1, 4 * rows), 1)
    txt_keys = jnp.zeros((1, 4 * rows), jnp.float32)
    for slot, (source, start) in enumerate(
        ((before_ref, rows), (own_ref, rows), (after_ref, rows), (pair_ref, block + rows))
    ):
        extra = source[start : start + EXTRA, :].astype(jnp.float32)
        keys = extra[0:1] * 256.0 + extra[1:2]
        txt_keys = jnp.where(lane >= slot * rows, keys, txt_keys)

    one = lax.broadcasted_iota(jnp.int32, (rows, 256), 0) == lax.broadcasted_iota(
        jnp.int32, (rows, 256), 1
    )
    one = jnp.where(one, 1.0, 0.0).astype(jnp.bfloat16)
    for slot, source in enumerate((pair_ref, img_ref)):
        columns[slot * rows : (slot + 1) * rows, :] = lax.dot_general(
            one,
            source[rows : rows + EXTRA, 0:256],
            (((1,), (1,)), ((), ())),
            preferred_element_type=jnp.float32,
        )

    scores[...] = lax.dot_general(
        imgs[...], txts[...], (((1,), (1,)), ((), ())), preferred_element_type=jnp.float32
    )

    def step(number, total):
        here = pl.ds(pl.multiple_of(number * CHUNK, CHUNK), CHUNK)
        column = columns[here, :]
        img_keys = column[:, 0:1] * 256.0 + column[:, 1:2]
        weights = (column[:, 2:3] + column[:, 3:4]) + column[:, 4:5]
        same = img_keys == txt_keys
        score = scale * scores[here, :] + shift
        argument = jnp.where(same, -score, score)
        small = jnp.exp(-jnp.abs(argument))
        penalty = jnp.maximum(argument, 0.0) + jnp.log1p(small)
        share = 1.0 / (1.0 + small)
        sigmoid = jnp.where(argument >= 0.0, share, small * share)
        scaled = weights * scale
        factors[here, :] = (jnp.where(same, -scaled, scaled) * sigmoid).astype(jnp.bfloat16)
        return total + weights * penalty

    total = lax.fori_loop(
        0, 2 * rows // CHUNK, step, jnp.zeros((CHUNK, 4 * rows), jnp.float32)
    )
    loss_part = jnp.sum(jnp.sum(total, 0, keepdims=True), 1, keepdims=True)
    weight_part = jnp.sum(weight_ref[...], 1, keepdims=True)
    place = lax.broadcasted_iota(jnp.int32, sums_ref.shape, 1)
    sums_ref[...] = jnp.where(
        place == 0, loss_part, jnp.where(place == 1, weight_part, 0.0)
    )


def grad_kernel(
    factors,
    pair_ref,
    after_ref,
    img_ref,
    before_ref,
    own_ref,
    pair_out,
    img_out,
    before_out,
    after_out,
    own_out,
    txts,
    imgs,
):
    rows = own_out.shape[0]
    stack_blocks(rows, pair_ref, after_ref, img_ref, before_ref, own_ref, txts, imgs)
    img_grads = jnp.dot(factors[...], txts[...], preferred_element_type=jnp.float32)
    img_grads = img_grads.astype(jnp.bfloat16)
    pair_out[0:rows, :] = img_grads[0:rows]
    img_out[...] = img_grads[rows : 2 * rows]
    txt_grads = lax.dot_general(
        factors[...], imgs[...], (((0,), (0,)), ((), ())), preferred_element_type=jnp.float32
    )
    before_out[...] = txt_grads[0:rows].astype(jnp.bfloat16)
    own_out[...] = txt_grads[rows : 2 * rows]
    after_out[...] = txt_grads[2 * rows : 3 * rows].astype(jnp.bfloat16)
    pair_out[rows : 2 * rows, :] = txt_grads[3 * rows : 4 * rows].astype(jnp.bfloat16)


def finish_kernel(
    img_ref, txt_ref, pair_ref, before_ref, far_ref, after_ref, own_ref, sums_ref,
    img_out, txt_out, loss_out
):
    rows = img_ref.shape[0]

    def finish(values, grad):
        norm = row_norms(values)
        unit = values / norm
        return (grad - unit * jnp.sum(unit * grad, -1, keepdims=True)) / norm

    wide = lambda part: part.astype(jnp.float32)
    img_out[...] = finish(img_ref[...], wide(pair_ref[0:rows, :]) + wide(far_ref[...]))
    txt_out[...] = finish(
        txt_ref[...],
        (own_ref[...] + wide(before_ref[...]))
        + (wide(after_ref[...]) + wide(pair_ref[rows : 2 * rows, :])),
    )
    sums = jnp.sum(sums_ref[...], 0, keepdims=True)
    loss_out[...] = sums[:, 0:1] / sums[:, 1:2]


def exchange(part, groups):
    count = len(groups[0])
    spread = jnp.broadcast_to(part.reshape(1, 1, -1), (count, 1, part.shape[-1]))
    return lax.all_to_all(
        spread, ("blk", "group"), 0, 0, tiled=True, axis_index_groups=groups
    ).reshape(count, -1)


def plane_and_column_groups():
    blk, group = lax.axis_size("blk"), lax.axis_size("group")
    planes, columns = {}, {}
    for number in range(blk * group):
        first, second = number // group, number % group
        z = (second % Z_HI, first // PLANE)
        planes.setdefault(z, []).append(number)
        columns.setdefault((first % PLANE, second // Z_HI), []).append(number)
    return list(planes.values()), list(columns.values())


def per_device(image_emb, text_emb, keys, weights, scale, shift):
    rows, width = image_emb.shape
    block = rows + EXTRA
    half = lambda *shape: jax.ShapeDtypeStruct(shape, jnp.bfloat16)
    full = lambda *shape: jax.ShapeDtypeStruct(shape, jnp.float32)
    smem = [pl.BlockSpec(memory_space=pltpu.SMEM)] * 2
    hbm = [pl.BlockSpec(memory_space=pltpu.HBM)] * 2
    row_weights = weights.reshape(1, rows)
    fixed = [pltpu.with_memory_space_constraint(x, pltpu.HBM) for x in (image_emb, text_emb)]
    pair, txt_block, img_block, txt_again = call(
        prepare_kernel,
        [half(2 * block, width)] + [half(block, width)] * 3,
        (*fixed, keys.reshape(1, rows), row_weights),
        hbm + vmem(2),
        [
            pltpu.VMEM((rows, width), jnp.float32),
            pltpu.VMEM((rows, width), jnp.float32),
            pltpu.SemaphoreType.DMA((2,)),
        ],
        6 * rows * width,
        0,
        16 * rows * width,
        VMEM_BYTES,
    )
    pair_ahead = from_ahead(pair, "blk", FAR)
    txt_after = from_ahead(txt_block, "blk", 1)
    img_behind = from_ahead(img_block, "blk", -FAR)
    txt_before = from_ahead(txt_again, "blk", -1)
    blocks = (pair_ahead, txt_after, img_behind, txt_before, txt_block)
    stacks = [
        pltpu.VMEM((4 * rows, width), jnp.bfloat16),
        pltpu.VMEM((2 * rows, width), jnp.bfloat16),
    ]
    sums, factors = call(
        score_kernel,
        [full(8, 128), half(2 * rows, 4 * rows)],
        (scale, shift, row_weights, *blocks),
        smem + vmem(6),
        stacks
        + [
            pltpu.VMEM((2 * rows, 4 * rows), jnp.float32),
            pltpu.VMEM((2 * rows, EXTRA), jnp.float32),
        ],
        16 * rows * rows * width,
        24 * rows * rows,
        28 * rows * width,
        VMEM_BYTES,
    )
    parts = call(
        grad_kernel,
        [
            half(2 * rows, width),
            half(rows, width),
            half(rows, width),
            half(rows, width),
            full(rows, width),
        ],
        (factors, *blocks),
        vmem(6),
        stacks,
        32 * rows * rows * width,
        0,
        28 * rows * width,
        VMEM_BYTES,
    )
    planes, columns = plane_and_column_groups()
    parts, sums = lax.optimization_barrier((parts, sums))
    gathered = exchange(sums[0:1], planes)
    parts, gathered = lax.optimization_barrier((parts, gathered))
    pair_part, img_part, before_part, after_part, own_part = parts
    pair_back = from_ahead(pair_part, "blk", -FAR)
    before_back = from_ahead(after_part, "blk", -1)
    far_back = from_ahead(img_part, "blk", FAR)
    after_back = from_ahead(before_part, "blk", 1)
    gathered = exchange(jnp.sum(gathered, 0, keepdims=True), columns)
    image_grad, text_grad, loss = call(
        finish_kernel,
        [full(rows, width), full(rows, width), full(1, 1)],
        (
            image_emb,
            text_emb,
            pair_back,
            before_back,
            far_back,
            after_back,
            own_part,
            gathered,
        ),
        vmem(8),
        [],
        20 * rows * width,
        0,
        30 * rows * width,
        VMEM_BYTES,
    )
    return (loss.reshape(1), image_grad, text_grad)


def solution(mesh):
    split = ("blk", "group")
    placed = (P(split, None), P(split, None), P(split), P(split), P(), P())
    return jax.shard_map(
        per_device,
        mesh=mesh,
        in_specs=placed,
        out_specs=(P(), P(split, None), P(split, None)),
        check_vma=False,
    )
```

```python
import jax
import jax.numpy as jnp
from jax import lax
from jax.experimental import pallas as pl
from jax.experimental.pallas import tpu as pltpu
from jax.sharding import PartitionSpec as P

EXTRA = 16
CHUNK = 32
VMEM_BYTES = 16 * 1024 * 1024
PLANE = 8
Z_HI = 4


def exchange_pairs(value, distance, keep):
    count = lax.axis_size("blk")
    pairs = []
    for first in range(count):
        if keep(first):
            second = (first + distance) % count
            pairs += [(first, second), (second, first)]
    return lax.ppermute(value, "blk", sorted(pairs))


def with_chip_inside(value):
    return exchange_pairs(value, 2, lambda first: first % 4 < 2)


def with_chip_across(value):
    return exchange_pairs(value, 2, lambda first: first % 4 >= 2)


def with_next_core(value):
    return exchange_pairs(value, 1, lambda first: first % 2 == 1)


def with_other_core(value):
    return exchange_pairs(value, 1, lambda first: first % 2 == 0)


def row_norms(values):
    return jnp.sqrt(jnp.sum(values * values, -1, keepdims=True) + 1e-06)


def vmem(count):
    return [pl.BlockSpec(memory_space=pltpu.VMEM)] * count


def call(kernel, outs, args, specs, scratch, flops, transcendentals, moved, limit):
    return pl.pallas_call(
        kernel,
        out_shape=outs,
        in_specs=specs,
        out_specs=vmem(len(outs)),
        scratch_shapes=scratch,
        compiler_params=pltpu.CompilerParams(vmem_limit_bytes=limit),
        cost_estimate=pl.CostEstimate(
            flops=flops, bytes_accessed=moved, transcendentals=transcendentals
        ),
    )(*args)


def prepare_kernel(
    img_ref, txt_ref, key_ref, weight_ref, pair_ref, txt_out, img_buf, txt_buf, sems
):
    rows, width = img_buf.shape
    block = rows + EXTRA
    copies = [
        pltpu.make_async_copy(source, target, sems.at[number])
        for number, (source, target) in enumerate(((img_ref, img_buf), (txt_ref, txt_buf)))
    ]
    for copy in copies:
        copy.start()
    key = key_ref[...]
    weight = weight_ref[...]
    high = weight.astype(jnp.bfloat16).astype(jnp.float32)
    middle = (weight - high).astype(jnp.bfloat16).astype(jnp.float32)
    low = (weight - high) - middle
    line = lax.broadcasted_iota(jnp.int32, (EXTRA, rows), 0)
    extra = jnp.zeros((EXTRA, rows), jnp.float32)
    parts = (
        (key >> 8).astype(jnp.float32),
        (key & 255).astype(jnp.float32),
        high,
        middle,
        low,
    )
    for number, part in enumerate(parts):
        extra = jnp.where(line == number, part, extra)
    place = lax.broadcasted_iota(jnp.int32, (rows, width), 1) - lax.broadcasted_iota(
        jnp.int32, (rows, width), 0
    )
    hit = place == 0
    for number in range(1, width // rows):
        hit = jnp.logical_or(hit, place == number * rows)
    extra = jnp.dot(
        extra.astype(jnp.bfloat16),
        jnp.where(hit, 1.0, 0.0).astype(jnp.bfloat16),
        preferred_element_type=jnp.float32,
    ).astype(jnp.bfloat16)
    for start, source, alone, copy in (
        (0, img_buf, (), copies[0]),
        (block, txt_buf, (txt_out,), copies[1]),
    ):
        copy.wait()
        values = source[...]
        unit = (values / row_norms(values)).astype(jnp.bfloat16)
        for target in (*alone, pair_ref.at[start : start + block]):
            target[0:rows, :] = unit
            target[rows:block, :] = extra


def stack_blocks(rows, odd_ref, inside_ref, across_ref, next_ref, other_ref, own_ref, txts, imgs):
    block = rows + EXTRA
    imgs[0:rows, :] = inside_ref[0:rows, :]
    imgs[rows : 2 * rows, :] = across_ref[0:rows, :]
    txts[0:rows, :] = next_ref[0:rows, :]
    txts[rows : 2 * rows, :] = own_ref[0:rows, :]
    txts[2 * rows : 3 * rows, :] = other_ref[0:rows, :]

    @pl.when(odd_ref[0] == 0)
    def _():
        txts[3 * rows : 4 * rows, :] = inside_ref[block : block + rows, :]

    @pl.when(odd_ref[0] == 1)
    def _():
        txts[3 * rows : 4 * rows, :] = across_ref[block : block + rows, :]


def score_kernel(
    scale_ref,
    shift_ref,
    odd_ref,
    weight_ref,
    inside_ref,
    across_ref,
    next_ref,
    other_ref,
    own_ref,
    sums_ref,
    factors,
    txts,
    imgs,
    scores,
    columns,
):
    rows = own_ref.shape[0] - EXTRA
    block = rows + EXTRA
    scale = scale_ref[0]
    shift = shift_ref[0]

    stack_blocks(rows, odd_ref, inside_ref, across_ref, next_ref, other_ref, own_ref, txts, imgs)

    lane = lax.broadcasted_iota(jnp.int32, (1, 4 * rows), 1)
    txt_keys = jnp.zeros((1, 4 * rows), jnp.float32)
    ahead = jnp.where(
        odd_ref[0] == 0,
        inside_ref[block + rows : 2 * block, :].astype(jnp.float32),
        across_ref[block + rows : 2 * block, :].astype(jnp.float32),
    )
    extras = [
        source[rows:block, :].astype(jnp.float32) for source in (next_ref, own_ref, other_ref)
    ]
    for slot, extra in enumerate((*extras, ahead)):
        keys = extra[0:1] * 256.0 + extra[1:2]
        txt_keys = jnp.where(lane >= slot * rows, keys, txt_keys)

    one = lax.broadcasted_iota(jnp.int32, (rows, 256), 0) == lax.broadcasted_iota(
        jnp.int32, (rows, 256), 1
    )
    one = jnp.where(one, 1.0, 0.0).astype(jnp.bfloat16)
    for slot, source in enumerate((inside_ref, across_ref)):
        columns[slot * rows : (slot + 1) * rows, :] = lax.dot_general(
            one,
            source[rows : rows + EXTRA, 0:256],
            (((1,), (1,)), ((), ())),
            preferred_element_type=jnp.float32,
        )

    scores[...] = lax.dot_general(
        imgs[...], txts[...], (((1,), (1,)), ((), ())), preferred_element_type=jnp.float32
    )

    def step(number, total):
        here = pl.ds(pl.multiple_of(number * CHUNK, CHUNK), CHUNK)
        column = columns[here, :]
        img_keys = column[:, 0:1] * 256.0 + column[:, 1:2]
        weights = (column[:, 2:3] + column[:, 3:4]) + column[:, 4:5]
        same = img_keys == txt_keys
        score = scale * scores[here, :] + shift
        argument = jnp.where(same, -score, score)
        small = jnp.exp(-jnp.abs(argument))
        penalty = jnp.maximum(argument, 0.0) + jnp.log1p(small)
        share = 1.0 / (1.0 + small)
        sigmoid = jnp.where(argument >= 0.0, share, small * share)
        scaled = weights * scale
        factors[here, :] = (jnp.where(same, -scaled, scaled) * sigmoid).astype(jnp.bfloat16)
        return total + weights * penalty

    total = lax.fori_loop(
        0, 2 * rows // CHUNK, step, jnp.zeros((CHUNK, 4 * rows), jnp.float32)
    )
    loss_part = jnp.sum(jnp.sum(total, 0, keepdims=True), 1, keepdims=True)
    weight_part = jnp.sum(weight_ref[...], 1, keepdims=True)
    place = lax.broadcasted_iota(jnp.int32, sums_ref.shape, 1)
    sums_ref[...] = jnp.where(
        place == 0, loss_part, jnp.where(place == 1, weight_part, 0.0)
    )


def grad_kernel(
    odd_ref,
    factors,
    inside_ref,
    across_ref,
    next_ref,
    other_ref,
    own_ref,
    inside_out,
    across_out,
    next_out,
    other_out,
    own_out,
    txts,
    imgs,
):
    rows = own_out.shape[0]
    stack_blocks(rows, odd_ref, inside_ref, across_ref, next_ref, other_ref, own_ref, txts, imgs)
    img_grads = jnp.dot(factors[...], txts[...], preferred_element_type=jnp.float32)
    img_grads = img_grads.astype(jnp.bfloat16)
    inside_out[0:rows, :] = img_grads[0:rows]
    across_out[0:rows, :] = img_grads[rows : 2 * rows]
    txt_grads = lax.dot_general(
        factors[...], imgs[...], (((0,), (0,)), ((), ())), preferred_element_type=jnp.float32
    )
    next_out[...] = txt_grads[0:rows].astype(jnp.bfloat16)
    own_out[...] = txt_grads[rows : 2 * rows]
    other_out[...] = txt_grads[2 * rows : 3 * rows].astype(jnp.bfloat16)
    odd = odd_ref[0].astype(jnp.float32)
    ahead = txt_grads[3 * rows : 4 * rows]
    inside_out[rows : 2 * rows, :] = (ahead * (1.0 - odd)).astype(jnp.bfloat16)
    across_out[rows : 2 * rows, :] = (ahead * odd).astype(jnp.bfloat16)


def finish_kernel(
    img_ref, txt_ref, across_ref, inside_ref, next_ref, other_ref, own_ref, sums_ref,
    img_out, txt_out, loss_out
):
    rows = img_ref.shape[0]

    def finish(values, grad):
        norm = row_norms(values)
        unit = values / norm
        return (grad - unit * jnp.sum(unit * grad, -1, keepdims=True)) / norm

    wide = lambda part: part.astype(jnp.float32)
    img_out[...] = finish(img_ref[...], wide(inside_ref[0:rows, :]) + wide(across_ref[0:rows, :]))
    txt_out[...] = finish(
        txt_ref[...],
        (own_ref[...] + wide(next_ref[...]))
        + (wide(other_ref[...]) + wide(inside_ref[rows : 2 * rows, :]))
        + wide(across_ref[rows : 2 * rows, :]),
    )
    sums = jnp.sum(sums_ref[...], 0, keepdims=True)
    loss_out[...] = sums[:, 0:1] / sums[:, 1:2]


def exchange(part, groups):
    count = len(groups[0])
    spread = jnp.broadcast_to(part.reshape(1, 1, -1), (count, 1, part.shape[-1]))
    return lax.all_to_all(
        spread, ("blk", "group"), 0, 0, tiled=True, axis_index_groups=groups
    ).reshape(count, -1)


def plane_and_column_groups():
    blk, group = lax.axis_size("blk"), lax.axis_size("group")
    planes, columns = {}, {}
    for number in range(blk * group):
        first, second = number // group, number % group
        z = (second % Z_HI, first // PLANE)
        planes.setdefault(z, []).append(number)
        columns.setdefault((first % PLANE, second // Z_HI), []).append(number)
    return list(planes.values()), list(columns.values())


def per_device(image_emb, text_emb, keys, weights, scale, shift):
    rows, width = image_emb.shape
    block = rows + EXTRA
    half = lambda *shape: jax.ShapeDtypeStruct(shape, jnp.bfloat16)
    full = lambda *shape: jax.ShapeDtypeStruct(shape, jnp.float32)
    smem = [pl.BlockSpec(memory_space=pltpu.SMEM)]
    hbm = [pl.BlockSpec(memory_space=pltpu.HBM)] * 2
    row_weights = weights.reshape(1, rows)
    fixed = [pltpu.with_memory_space_constraint(x, pltpu.HBM) for x in (image_emb, text_emb)]
    pair, txt_block = call(
        prepare_kernel,
        [half(2 * block, width), half(block, width)],
        (*fixed, keys.reshape(1, rows), row_weights),
        hbm + vmem(2),
        [
            pltpu.VMEM((rows, width), jnp.float32),
            pltpu.VMEM((rows, width), jnp.float32),
            pltpu.SemaphoreType.DMA((2,)),
        ],
        6 * rows * width,
        0,
        16 * rows * width,
        VMEM_BYTES,
    )
    odd = ((lax.axis_index("blk") >> 1) & 1).astype(jnp.int32).reshape(1)
    across = with_chip_across(pair)
    inside = with_chip_inside(pair)
    next_core = with_next_core(txt_block)
    other_core = with_other_core(txt_block)
    blocks = (inside, across, next_core, other_core, txt_block)
    stacks = [
        pltpu.VMEM((4 * rows, width), jnp.bfloat16),
        pltpu.VMEM((2 * rows, width), jnp.bfloat16),
    ]
    sums, factors = call(
        score_kernel,
        [full(8, 128), half(2 * rows, 4 * rows)],
        (scale, shift, odd, row_weights, *blocks),
        smem * 3 + vmem(6),
        stacks
        + [
            pltpu.VMEM((2 * rows, 4 * rows), jnp.float32),
            pltpu.VMEM((2 * rows, EXTRA), jnp.float32),
        ],
        16 * rows * rows * width,
        24 * rows * rows,
        28 * rows * width,
        VMEM_BYTES,
    )
    parts = call(
        grad_kernel,
        [
            half(2 * rows, width),
            half(2 * rows, width),
            half(rows, width),
            half(rows, width),
            full(rows, width),
        ],
        (odd, factors, *blocks),
        smem + vmem(6),
        stacks,
        32 * rows * rows * width,
        0,
        28 * rows * width,
        VMEM_BYTES,
    )
    planes, columns = plane_and_column_groups()
    gathered = exchange(sums[0:1], planes)
    inside_part, across_part, next_part, other_part, own_part = parts
    across_back = with_chip_across(across_part)
    inside_back = with_chip_inside(inside_part)
    next_back = with_next_core(next_part)
    other_back = with_other_core(other_part)
    gathered = exchange(jnp.sum(gathered, 0, keepdims=True), columns)
    image_grad, text_grad, loss = call(
        finish_kernel,
        [full(rows, width), full(rows, width), full(1, 1)],
        (
            image_emb,
            text_emb,
            across_back,
            inside_back,
            next_back,
            other_back,
            own_part,
            gathered,
        ),
        vmem(8),
        [],
        20 * rows * width,
        0,
        30 * rows * width,
        VMEM_BYTES,
    )
    return (loss.reshape(1), image_grad, text_grad)


def solution(mesh):
    split = ("blk", "group")
    placed = (P(split, None), P(split, None), P(split), P(split), P(), P())
    return jax.shard_map(
        per_device,
        mesh=mesh,
        in_specs=placed,
        out_specs=(P(), P(split, None), P(split, None)),
        check_vma=False,
    )
```

```python
import jax
import jax.numpy as jnp
from jax import lax
from jax.experimental import pallas as pl
from jax.experimental.pallas import tpu as pltpu
from jax.sharding import PartitionSpec as P

EXTRA = 16
CHUNK = 32
VMEM_BYTES = 16 * 1024 * 1024
PLANE = 8
Z_HI = 4


def exchange_pairs(value, distance, keep):
    count = lax.axis_size("blk")
    pairs = []
    for first in range(count):
        if keep(first):
            second = (first + distance) % count
            pairs += [(first, second), (second, first)]
    return lax.ppermute(value, "blk", sorted(pairs))


def with_chip_inside(value):
    return exchange_pairs(value, 2, lambda first: first % 4 < 2)


def with_chip_across(value):
    return exchange_pairs(value, 2, lambda first: first % 4 >= 2)


def with_next_core(value):
    return exchange_pairs(value, 1, lambda first: first % 2 == 1)


def with_other_core(value):
    return exchange_pairs(value, 1, lambda first: first % 2 == 0)


def row_norms(values):
    return jnp.sqrt(jnp.sum(values * values, -1, keepdims=True) + 1e-06)


def vmem(count):
    return [pl.BlockSpec(memory_space=pltpu.VMEM)] * count


def call(kernel, outs, args, specs, scratch, flops, transcendentals, moved, limit):
    return pl.pallas_call(
        kernel,
        out_shape=outs,
        in_specs=specs,
        out_specs=vmem(len(outs)),
        scratch_shapes=scratch,
        compiler_params=pltpu.CompilerParams(vmem_limit_bytes=limit),
        cost_estimate=pl.CostEstimate(
            flops=flops, bytes_accessed=moved, transcendentals=transcendentals
        ),
    )(*args)


def prepare_kernel(
    img_ref, txt_ref, key_ref, weight_ref, pair_ref, txt_out, img_buf, txt_buf, sems
):
    rows, width = img_buf.shape
    block = rows + EXTRA
    copies = [
        pltpu.make_async_copy(source, target, sems.at[number])
        for number, (source, target) in enumerate(((img_ref, img_buf), (txt_ref, txt_buf)))
    ]
    for copy in copies:
        copy.start()
    key = key_ref[...]
    weight = weight_ref[...]
    high = weight.astype(jnp.bfloat16).astype(jnp.float32)
    middle = (weight - high).astype(jnp.bfloat16).astype(jnp.float32)
    low = (weight - high) - middle
    line = lax.broadcasted_iota(jnp.int32, (EXTRA, rows), 0)
    extra = jnp.zeros((EXTRA, rows), jnp.float32)
    parts = (
        (key >> 8).astype(jnp.float32),
        (key & 255).astype(jnp.float32),
        high,
        middle,
        low,
    )
    for number, part in enumerate(parts):
        extra = jnp.where(line == number, part, extra)
    place = lax.broadcasted_iota(jnp.int32, (rows, width), 1) - lax.broadcasted_iota(
        jnp.int32, (rows, width), 0
    )
    hit = place == 0
    for number in range(1, width // rows):
        hit = jnp.logical_or(hit, place == number * rows)
    extra = jnp.dot(
        extra.astype(jnp.bfloat16),
        jnp.where(hit, 1.0, 0.0).astype(jnp.bfloat16),
        preferred_element_type=jnp.float32,
    ).astype(jnp.bfloat16)
    for start, source, alone, copy in (
        (0, img_buf, (), copies[0]),
        (block, txt_buf, (txt_out,), copies[1]),
    ):
        copy.wait()
        values = source[...]
        unit = (values / row_norms(values)).astype(jnp.bfloat16)
        for target in (*alone, pair_ref.at[start : start + block]):
            target[0:rows, :] = unit
            target[rows:block, :] = extra


def stack_blocks(
    rows, odd_ref, inside_ref, across_ref, next_ref, other_ref, own_ref, txts, imgs, tails, sems
):
    block = rows + EXTRA
    copies = []
    for number, source in enumerate((next_ref, other_ref)):
        copies += [
            pltpu.make_async_copy(
                source.at[0:rows],
                txts.at[2 * number * rows : (2 * number + 1) * rows],
                sems.at[2 * number],
            ),
            pltpu.make_async_copy(
                source.at[rows:block], tails.at[number], sems.at[2 * number + 1]
            ),
        ]
    for copy in copies:
        copy.start()
    imgs[0:rows, :] = inside_ref[0:rows, :]
    imgs[rows : 2 * rows, :] = across_ref[0:rows, :]
    txts[rows : 2 * rows, :] = own_ref[0:rows, :]

    @pl.when(odd_ref[0] == 0)
    def _():
        txts[3 * rows : 4 * rows, :] = inside_ref[block : block + rows, :]

    @pl.when(odd_ref[0] == 1)
    def _():
        txts[3 * rows : 4 * rows, :] = across_ref[block : block + rows, :]

    for copy in copies:
        copy.wait()


def tile_kernel(
    scale_ref,
    shift_ref,
    odd_ref,
    weight_ref,
    inside_ref,
    across_ref,
    next_ref,
    other_ref,
    own_ref,
    sums_ref,
    inside_out,
    across_out,
    next_out,
    other_out,
    own_out,
    factors,
    txts,
    imgs,
    scores,
    columns,
    tails,
    sems,
):
    rows = own_ref.shape[0] - EXTRA
    block = rows + EXTRA
    scale = scale_ref[0]
    shift = shift_ref[0]

    stack_blocks(rows, odd_ref, inside_ref, across_ref, next_ref, other_ref, own_ref, txts, imgs, tails, sems)

    lane = lax.broadcasted_iota(jnp.int32, (1, 4 * rows), 1)
    txt_keys = jnp.zeros((1, 4 * rows), jnp.float32)
    ahead = jnp.where(
        odd_ref[0] == 0,
        inside_ref[block + rows : 2 * block, :].astype(jnp.float32),
        across_ref[block + rows : 2 * block, :].astype(jnp.float32),
    )
    extras = [
        part.astype(jnp.float32) for part in (tails[0], own_ref[rows:block, :], tails[1])
    ]
    for slot, extra in enumerate((*extras, ahead)):
        keys = extra[0:1] * 256.0 + extra[1:2]
        txt_keys = jnp.where(lane >= slot * rows, keys, txt_keys)

    one = lax.broadcasted_iota(jnp.int32, (rows, 256), 0) == lax.broadcasted_iota(
        jnp.int32, (rows, 256), 1
    )
    one = jnp.where(one, 1.0, 0.0).astype(jnp.bfloat16)
    for slot, source in enumerate((inside_ref, across_ref)):
        columns[slot * rows : (slot + 1) * rows, :] = lax.dot_general(
            one,
            source[rows : rows + EXTRA, 0:256],
            (((1,), (1,)), ((), ())),
            preferred_element_type=jnp.float32,
        )

    scores[...] = lax.dot_general(
        imgs[...], txts[...], (((1,), (1,)), ((), ())), preferred_element_type=jnp.float32
    )

    def step(number, total):
        here = pl.ds(pl.multiple_of(number * CHUNK, CHUNK), CHUNK)
        column = columns[here, :]
        img_keys = column[:, 0:1] * 256.0 + column[:, 1:2]
        weights = (column[:, 2:3] + column[:, 3:4]) + column[:, 4:5]
        same = img_keys == txt_keys
        score = scale * scores[here, :] + shift
        argument = jnp.where(same, -score, score)
        small = jnp.exp(-jnp.abs(argument))
        penalty = jnp.maximum(argument, 0.0) + jnp.log1p(small)
        share = 1.0 / (1.0 + small)
        sigmoid = jnp.where(argument >= 0.0, share, small * share)
        scaled = weights * scale
        factors[here, :] = (jnp.where(same, -scaled, scaled) * sigmoid).astype(jnp.bfloat16)
        return total + weights * penalty

    total = lax.fori_loop(
        0, 2 * rows // CHUNK, step, jnp.zeros((CHUNK, 4 * rows), jnp.float32)
    )
    loss_part = jnp.sum(jnp.sum(total, 0, keepdims=True), 1, keepdims=True)
    weight_part = jnp.sum(weight_ref[...], 1, keepdims=True)
    place = lax.broadcasted_iota(jnp.int32, sums_ref.shape, 1)
    sums_ref[...] = jnp.where(
        place == 0, loss_part, jnp.where(place == 1, weight_part, 0.0)
    )

    img_grads = jnp.dot(factors[...], txts[...], preferred_element_type=jnp.float32)
    img_grads = img_grads.astype(jnp.bfloat16)
    inside_out[0:rows, :] = img_grads[0:rows]
    across_out[0:rows, :] = img_grads[rows : 2 * rows]
    txt_grads = lax.dot_general(
        factors[...], imgs[...], (((0,), (0,)), ((), ())), preferred_element_type=jnp.float32
    )
    next_out[...] = txt_grads[0:rows].astype(jnp.bfloat16)
    own_out[...] = txt_grads[rows : 2 * rows]
    other_out[...] = txt_grads[2 * rows : 3 * rows].astype(jnp.bfloat16)
    odd = odd_ref[0].astype(jnp.float32)
    ahead = txt_grads[3 * rows : 4 * rows]
    inside_out[rows : 2 * rows, :] = (ahead * (1.0 - odd)).astype(jnp.bfloat16)
    across_out[rows : 2 * rows, :] = (ahead * odd).astype(jnp.bfloat16)


def finish_kernel(
    img_ref, txt_ref, across_ref, inside_ref, next_ref, other_ref, own_ref, sums_ref,
    img_out, txt_out, loss_out
):
    rows = img_ref.shape[0]

    def finish(values, grad):
        norm = row_norms(values)
        unit = values / norm
        return (grad - unit * jnp.sum(unit * grad, -1, keepdims=True)) / norm

    wide = lambda part: part.astype(jnp.float32)
    img_out[...] = finish(img_ref[...], wide(inside_ref[0:rows, :]) + wide(across_ref[0:rows, :]))
    txt_out[...] = finish(
        txt_ref[...],
        (own_ref[...] + wide(next_ref[...]))
        + (wide(other_ref[...]) + wide(inside_ref[rows : 2 * rows, :]))
        + wide(across_ref[rows : 2 * rows, :]),
    )
    sums = jnp.sum(sums_ref[...], 0, keepdims=True)
    loss_out[...] = sums[:, 0:1] / sums[:, 1:2]


def exchange(part, groups):
    count = len(groups[0])
    spread = jnp.broadcast_to(part.reshape(1, 1, -1), (count, 1, part.shape[-1]))
    return lax.all_to_all(
        spread, ("blk", "group"), 0, 0, tiled=True, axis_index_groups=groups
    ).reshape(count, -1)


def plane_and_column_groups():
    blk, group = lax.axis_size("blk"), lax.axis_size("group")
    planes, columns = {}, {}
    for number in range(blk * group):
        first, second = number // group, number % group
        z = (second % Z_HI, first // PLANE)
        planes.setdefault(z, []).append(number)
        columns.setdefault((first % PLANE, second // Z_HI), []).append(number)
    return list(planes.values()), list(columns.values())


def per_device(image_emb, text_emb, keys, weights, scale, shift):
    rows, width = image_emb.shape
    block = rows + EXTRA
    half = lambda *shape: jax.ShapeDtypeStruct(shape, jnp.bfloat16)
    full = lambda *shape: jax.ShapeDtypeStruct(shape, jnp.float32)
    smem = [pl.BlockSpec(memory_space=pltpu.SMEM)]
    hbm = [pl.BlockSpec(memory_space=pltpu.HBM)] * 2
    row_weights = weights.reshape(1, rows)
    fixed = [pltpu.with_memory_space_constraint(x, pltpu.HBM) for x in (image_emb, text_emb)]
    pair, txt_block = call(
        prepare_kernel,
        [half(2 * block, width), half(block, width)],
        (*fixed, keys.reshape(1, rows), row_weights),
        hbm + vmem(2),
        [
            pltpu.VMEM((rows, width), jnp.float32),
            pltpu.VMEM((rows, width), jnp.float32),
            pltpu.SemaphoreType.DMA((2,)),
        ],
        6 * rows * width,
        0,
        16 * rows * width,
        VMEM_BYTES,
    )
    odd = ((lax.axis_index("blk") >> 1) & 1).astype(jnp.int32).reshape(1)
    across = with_chip_across(pair)
    inside = with_chip_inside(pair)
    next_core = with_next_core(txt_block)
    other_core = with_other_core(txt_block)
    near = [pltpu.with_memory_space_constraint(x, pltpu.HBM) for x in (next_core, other_core)]
    blocks = (inside, across, *near, txt_block)
    sums, *parts = call(
        tile_kernel,
        [
            full(8, 128),
            half(2 * rows, width),
            half(2 * rows, width),
            half(rows, width),
            half(rows, width),
            full(rows, width),
        ],
        (scale, shift, odd, row_weights, *blocks),
        smem * 3 + vmem(3) + hbm + vmem(1),
        [
            pltpu.VMEM((2 * rows, 4 * rows), jnp.bfloat16),
            pltpu.VMEM((4 * rows, width), jnp.bfloat16),
            pltpu.VMEM((2 * rows, width), jnp.bfloat16),
            pltpu.VMEM((2 * rows, 4 * rows), jnp.float32),
            pltpu.VMEM((2 * rows, EXTRA), jnp.float32),
            pltpu.VMEM((2, EXTRA, width), jnp.bfloat16),
            pltpu.SemaphoreType.DMA((4,)),
        ],
        48 * rows * rows * width,
        24 * rows * rows,
        40 * rows * width,
        VMEM_BYTES,
    )
    planes, columns = plane_and_column_groups()
    gathered = exchange(sums[0:1], planes)
    inside_part, across_part, next_part, other_part, own_part = parts
    across_back = with_chip_across(across_part)
    inside_back = with_chip_inside(inside_part)
    next_back = with_next_core(next_part)
    other_back = with_other_core(other_part)
    gathered = exchange(jnp.sum(gathered, 0, keepdims=True), columns)
    image_grad, text_grad, loss = call(
        finish_kernel,
        [full(rows, width), full(rows, width), full(1, 1)],
        (
            image_emb,
            text_emb,
            across_back,
            inside_back,
            next_back,
            other_back,
            own_part,
            gathered,
        ),
        vmem(8),
        [],
        20 * rows * width,
        0,
        30 * rows * width,
        VMEM_BYTES,
    )
    return (loss.reshape(1), image_grad, text_grad)


def solution(mesh):
    split = ("blk", "group")
    placed = (P(split, None), P(split, None), P(split), P(split), P(), P())
    return jax.shard_map(
        per_device,
        mesh=mesh,
        in_specs=placed,
        out_specs=(P(), P(split, None), P(split, None)),
        check_vma=False,
    )
```

```python
import jax
import jax.numpy as jnp
from jax import lax
from jax.experimental import pallas as pl
from jax.experimental.pallas import tpu as pltpu
from jax.sharding import PartitionSpec as P

EXTRA = 16
CHUNK = 32
VMEM_BYTES = 16 * 1024 * 1024
PLANE = 8
Z_HI = 4


def exchange_pairs(value, distance, keep):
    count = lax.axis_size("blk")
    pairs = []
    for first in range(count):
        if keep(first):
            second = (first + distance) % count
            pairs += [(first, second), (second, first)]
    return lax.ppermute(value, "blk", sorted(pairs))


def with_chip_inside(value):
    return exchange_pairs(value, 2, lambda first: first % 4 < 2)


def with_chip_across(value):
    return exchange_pairs(value, 2, lambda first: first % 4 >= 2)


def with_next_core(value):
    return exchange_pairs(value, 1, lambda first: first % 2 == 1)


def with_other_core(value):
    return exchange_pairs(value, 1, lambda first: first % 2 == 0)


def row_norms(values):
    return jnp.sqrt(jnp.sum(values * values, -1, keepdims=True) + 1e-06)


def vmem(count):
    return [pl.BlockSpec(memory_space=pltpu.VMEM)] * count


def call(kernel, outs, args, specs, scratch, flops, transcendentals, moved, limit):
    return pl.pallas_call(
        kernel,
        out_shape=outs,
        in_specs=specs,
        out_specs=vmem(len(outs)),
        scratch_shapes=scratch,
        compiler_params=pltpu.CompilerParams(vmem_limit_bytes=limit),
        cost_estimate=pl.CostEstimate(
            flops=flops, bytes_accessed=moved, transcendentals=transcendentals
        ),
    )(*args)


def prepare_kernel(
    img_ref, txt_ref, key_ref, weight_ref, pair_ref, txt_out, img_buf, txt_buf, sems
):
    rows, width = img_buf.shape
    block = rows + EXTRA
    copies = [
        pltpu.make_async_copy(source, target, sems.at[number])
        for number, (source, target) in enumerate(((img_ref, img_buf), (txt_ref, txt_buf)))
    ]
    for copy in copies:
        copy.start()
    key = key_ref[...]
    weight = weight_ref[...]
    high = weight.astype(jnp.bfloat16).astype(jnp.float32)
    middle = (weight - high).astype(jnp.bfloat16).astype(jnp.float32)
    low = (weight - high) - middle
    line = lax.broadcasted_iota(jnp.int32, (EXTRA, rows), 0)
    extra = jnp.zeros((EXTRA, rows), jnp.float32)
    parts = (
        (key >> 8).astype(jnp.float32),
        (key & 255).astype(jnp.float32),
        high,
        middle,
        low,
    )
    for number, part in enumerate(parts):
        extra = jnp.where(line == number, part, extra)
    place = lax.broadcasted_iota(jnp.int32, (rows, width), 1) - lax.broadcasted_iota(
        jnp.int32, (rows, width), 0
    )
    hit = place == 0
    for number in range(1, width // rows):
        hit = jnp.logical_or(hit, place == number * rows)
    extra = jnp.dot(
        extra.astype(jnp.bfloat16),
        jnp.where(hit, 1.0, 0.0).astype(jnp.bfloat16),
        preferred_element_type=jnp.float32,
    ).astype(jnp.bfloat16)
    for start, source, alone, copy in (
        (0, img_buf, (), copies[0]),
        (block, txt_buf, (txt_out,), copies[1]),
    ):
        copy.wait()
        values = source[...]
        unit = (values / row_norms(values)).astype(jnp.bfloat16)
        for target in (*alone, pair_ref.at[start : start + block]):
            target[0:rows, :] = unit
            target[rows:block, :] = extra


def stack_blocks(
    rows, odd_ref, inside_ref, across_ref, next_ref, other_ref, own_ref, txts, imgs, tails, sems
):
    block = rows + EXTRA
    copies = []
    for number, source in enumerate((next_ref, other_ref)):
        copies += [
            pltpu.make_async_copy(
                source.at[0:rows],
                txts.at[2 * number * rows : (2 * number + 1) * rows],
                sems.at[2 * number],
            ),
            pltpu.make_async_copy(
                source.at[rows:block], tails.at[number], sems.at[2 * number + 1]
            ),
        ]
    for copy in copies:
        copy.start()
    imgs[0:rows, :] = inside_ref[0:rows, :]
    imgs[rows : 2 * rows, :] = across_ref[0:rows, :]
    txts[rows : 2 * rows, :] = own_ref[0:rows, :]

    @pl.when(odd_ref[0] == 0)
    def _():
        txts[3 * rows : 4 * rows, :] = inside_ref[block : block + rows, :]

    @pl.when(odd_ref[0] == 1)
    def _():
        txts[3 * rows : 4 * rows, :] = across_ref[block : block + rows, :]

    for copy in copies:
        copy.wait()


def tile_kernel(
    scale_ref,
    shift_ref,
    odd_ref,
    weight_ref,
    inside_ref,
    across_ref,
    next_ref,
    other_ref,
    own_ref,
    sums_ref,
    inside_out,
    across_out,
    next_out,
    other_out,
    own_out,
    factors,
    txts,
    imgs,
    scores,
    columns,
    tails,
    sems,
):
    rows = own_ref.shape[0] - EXTRA
    block = rows + EXTRA
    scale = scale_ref[0]
    shift = shift_ref[0]

    stack_blocks(rows, odd_ref, inside_ref, across_ref, next_ref, other_ref, own_ref, txts, imgs, tails, sems)

    lane = lax.broadcasted_iota(jnp.int32, (1, 4 * rows), 1)
    txt_keys = jnp.zeros((1, 4 * rows), jnp.float32)
    ahead = jnp.where(
        odd_ref[0] == 0,
        inside_ref[block + rows : 2 * block, :].astype(jnp.float32),
        across_ref[block + rows : 2 * block, :].astype(jnp.float32),
    )
    extras = [
        part.astype(jnp.float32) for part in (tails[0], own_ref[rows:block, :], tails[1])
    ]
    for slot, extra in enumerate((*extras, ahead)):
        keys = extra[0:1] * 256.0 + extra[1:2]
        txt_keys = jnp.where(lane >= slot * rows, keys, txt_keys)

    one = lax.broadcasted_iota(jnp.int32, (rows, 256), 0) == lax.broadcasted_iota(
        jnp.int32, (rows, 256), 1
    )
    one = jnp.where(one, 1.0, 0.0).astype(jnp.bfloat16)
    for slot, source in enumerate((inside_ref, across_ref)):
        columns[slot * rows : (slot + 1) * rows, :] = lax.dot_general(
            one,
            source[rows : rows + EXTRA, 0:256],
            (((1,), (1,)), ((), ())),
            preferred_element_type=jnp.float32,
        )

    scores[...] = lax.dot_general(
        imgs[...], txts[...], (((1,), (1,)), ((), ())), preferred_element_type=jnp.float32
    )

    def step(number, total):
        here = pl.ds(pl.multiple_of(number * CHUNK, CHUNK), CHUNK)
        column = columns[here, :]
        img_keys = column[:, 0:1] * 256.0 + column[:, 1:2]
        weights = (column[:, 2:3] + column[:, 3:4]) + column[:, 4:5]
        same = img_keys == txt_keys
        score = scale * scores[here, :] + shift
        argument = jnp.where(same, -score, score)
        small = jnp.exp(-jnp.abs(argument))
        penalty = jnp.maximum(argument, 0.0) + jnp.log1p(small)
        share = 1.0 / (1.0 + small)
        sigmoid = jnp.where(argument >= 0.0, share, small * share)
        scaled = weights * scale
        factors[here, :] = (jnp.where(same, -scaled, scaled) * sigmoid).astype(jnp.bfloat16)
        return total + weights * penalty

    total = lax.fori_loop(
        0, 2 * rows // CHUNK, step, jnp.zeros((CHUNK, 4 * rows), jnp.float32), unroll=3
    )
    loss_part = jnp.sum(jnp.sum(total, 0, keepdims=True), 1, keepdims=True)
    weight_part = jnp.sum(weight_ref[...], 1, keepdims=True)
    place = lax.broadcasted_iota(jnp.int32, sums_ref.shape, 1)
    sums_ref[...] = jnp.where(
        place == 0, loss_part, jnp.where(place == 1, weight_part, 0.0)
    )

    img_grads = jnp.dot(factors[...], txts[...], preferred_element_type=jnp.float32)
    img_grads = img_grads.astype(jnp.bfloat16)
    inside_out[0:rows, :] = img_grads[0:rows]
    across_out[0:rows, :] = img_grads[rows : 2 * rows]
    txt_grads = lax.dot_general(
        factors[...], imgs[...], (((0,), (0,)), ((), ())), preferred_element_type=jnp.float32
    )
    next_out[...] = txt_grads[0:rows].astype(jnp.bfloat16)
    own_out[...] = txt_grads[rows : 2 * rows]
    other_out[...] = txt_grads[2 * rows : 3 * rows].astype(jnp.bfloat16)
    odd = odd_ref[0].astype(jnp.float32)
    ahead = txt_grads[3 * rows : 4 * rows]
    inside_out[rows : 2 * rows, :] = (ahead * (1.0 - odd)).astype(jnp.bfloat16)
    across_out[rows : 2 * rows, :] = (ahead * odd).astype(jnp.bfloat16)


def finish_kernel(
    img_ref, txt_ref, across_ref, inside_ref, next_ref, other_ref, own_ref, sums_ref,
    img_out, txt_out, loss_out
):
    rows = img_ref.shape[0]

    def finish(values, grad):
        norm = row_norms(values)
        unit = values / norm
        return (grad - unit * jnp.sum(unit * grad, -1, keepdims=True)) / norm

    wide = lambda part: part.astype(jnp.float32)
    img_out[...] = finish(img_ref[...], wide(inside_ref[0:rows, :]) + wide(across_ref[0:rows, :]))
    txt_out[...] = finish(
        txt_ref[...],
        (own_ref[...] + wide(next_ref[...]))
        + (wide(other_ref[...]) + wide(inside_ref[rows : 2 * rows, :]))
        + wide(across_ref[rows : 2 * rows, :]),
    )
    sums = jnp.sum(sums_ref[...], 0, keepdims=True)
    loss_out[...] = sums[:, 0:1] / sums[:, 1:2]


def spread_kernel(rows_ref, sum_ref):
    total = jnp.sum(rows_ref[...], 0, keepdims=True)
    sum_ref[...] = jnp.broadcast_to(total, sum_ref.shape)


def exchange(spread, groups):
    return lax.all_to_all(
        spread, ("blk", "group"), 0, 0, tiled=True, axis_index_groups=groups
    )


def plane_and_column_groups():
    blk, group = lax.axis_size("blk"), lax.axis_size("group")
    planes, columns = {}, {}
    for number in range(blk * group):
        first, second = number // group, number % group
        z = (second % Z_HI, first // PLANE)
        planes.setdefault(z, []).append(number)
        columns.setdefault((first % PLANE, second // Z_HI), []).append(number)
    return list(planes.values()), list(columns.values())


def per_device(image_emb, text_emb, keys, weights, scale, shift):
    rows, width = image_emb.shape
    block = rows + EXTRA
    half = lambda *shape: jax.ShapeDtypeStruct(shape, jnp.bfloat16)
    full = lambda *shape: jax.ShapeDtypeStruct(shape, jnp.float32)
    smem = [pl.BlockSpec(memory_space=pltpu.SMEM)]
    hbm = [pl.BlockSpec(memory_space=pltpu.HBM)] * 2
    row_weights = weights.reshape(1, rows)
    fixed = [pltpu.with_memory_space_constraint(x, pltpu.HBM) for x in (image_emb, text_emb)]
    pair, txt_block = call(
        prepare_kernel,
        [half(2 * block, width), half(block, width)],
        (*fixed, keys.reshape(1, rows), row_weights),
        hbm + vmem(2),
        [
            pltpu.VMEM((rows, width), jnp.float32),
            pltpu.VMEM((rows, width), jnp.float32),
            pltpu.SemaphoreType.DMA((2,)),
        ],
        6 * rows * width,
        0,
        16 * rows * width,
        VMEM_BYTES,
    )
    odd = ((lax.axis_index("blk") >> 1) & 1).astype(jnp.int32).reshape(1)
    across = with_chip_across(pair)
    inside = with_chip_inside(pair)
    next_core = with_next_core(txt_block)
    other_core = with_other_core(txt_block)
    near = [pltpu.with_memory_space_constraint(x, pltpu.HBM) for x in (next_core, other_core)]
    blocks = (inside, across, *near, txt_block)
    sums, *parts = call(
        tile_kernel,
        [
            full(8, 128),
            half(2 * rows, width),
            half(2 * rows, width),
            half(rows, width),
            half(rows, width),
            full(rows, width),
        ],
        (scale, shift, odd, row_weights, *blocks),
        smem * 3 + vmem(3) + hbm + vmem(1),
        [
            pltpu.VMEM((2 * rows, 4 * rows), jnp.bfloat16),
            pltpu.VMEM((4 * rows, width), jnp.bfloat16),
            pltpu.VMEM((2 * rows, width), jnp.bfloat16),
            pltpu.VMEM((2 * rows, 4 * rows), jnp.float32),
            pltpu.VMEM((2 * rows, EXTRA), jnp.float32),
            pltpu.VMEM((2, EXTRA, width), jnp.bfloat16),
            pltpu.SemaphoreType.DMA((4,)),
        ],
        48 * rows * rows * width,
        24 * rows * rows,
        40 * rows * width,
        VMEM_BYTES,
    )
    planes, columns = plane_and_column_groups()
    first = jnp.broadcast_to(sums[0:1].reshape(1, 1, -1), (len(planes[0]), 1, sums.shape[1]))
    gathered = exchange(first, planes)
    inside_part, across_part, next_part, other_part, own_part = parts
    across_back = with_chip_across(across_part)
    inside_back = with_chip_inside(inside_part)
    next_back = with_next_core(next_part)
    other_back = with_other_core(other_part)
    (second,) = call(
        spread_kernel,
        [full(len(columns[0]), 1, sums.shape[1])],
        (gathered,),
        vmem(1),
        [],
        4096,
        0,
        32768,
        VMEM_BYTES,
    )
    gathered = exchange(second, columns).reshape(len(columns[0]), -1)
    image_grad, text_grad, loss = call(
        finish_kernel,
        [full(rows, width), full(rows, width), full(1, 1)],
        (
            image_emb,
            text_emb,
            across_back,
            inside_back,
            next_back,
            other_back,
            own_part,
            gathered,
        ),
        vmem(8),
        [],
        20 * rows * width,
        0,
        30 * rows * width,
        VMEM_BYTES,
    )
    return (loss.reshape(1), image_grad, text_grad)


def solution(mesh):
    split = ("blk", "group")
    placed = (P(split, None), P(split, None), P(split), P(split), P(), P())
    return jax.shard_map(
        per_device,
        mesh=mesh,
        in_specs=placed,
        out_specs=(P(), P(split, None), P(split, None)),
        check_vma=False,
    )
```
